32 devices in a mesh: dp: 32 (over z, y, x, core).
Axes of the slice: x: 2, y: 2, z: 4, core: 2. Of those that a mesh axis runs over, the one named last changes fastest.
Arguments:
- tokens: bfloat16 [16384, 1024], P('dp'), may hold values from -6 to 6
- segments: int32 [16384], P('dp'), may hold values from 0 to 64, as said below
- norm_gain: bfloat16 [1024], P('dp'), may hold values from 0.25 to 1.75
- q_weight: bfloat16 [1024, 2048], P('dp'), may hold values from -0.1875 to 0.1875
- k_weight: bfloat16 [1024, 1024], P('dp'), may hold values from -0.1875 to 0.1875
- v_weight: bfloat16 [1024, 1024], P('dp'), may hold values from -0.1875 to 0.1875
- o_weight: bfloat16 [1024, 2048], P('dp'), may hold values from -1 to 1
- q_gain: bfloat16 [128], P('dp'), may hold values from 0.25 to 1.75
- k_gain: bfloat16 [128], P('dp'), may hold values from 0.25 to 1.75
- mlp_gain: bfloat16 [1024], P('dp'), may hold values from 0.25 to 1.75
- gate_weight: bfloat16 [1024, 3072], P('dp'), may hold values from -0.1875 to 0.1875
- up_weight: bfloat16 [1024, 3072], P('dp'), may hold values from -0.1875 to 0.1875
- down_weight: bfloat16 [1024, 3072], P('dp'), may hold values from -0.109375 to 0.109375
- cotangent: bfloat16 [16384, 1024], P('dp'), may hold values from -6 to 6
Outputs:
- mixed_out: bfloat16 [16384, 1024], P('dp')
- tokens_grad: bfloat16 [16384, 1024], P('dp')
- norm_gain_grad: float32 [1024], P('dp')
- q_weight_grad: float32 [1024, 2048], P('dp')
- k_weight_grad: float32 [1024, 1024], P('dp')
- v_weight_grad: float32 [1024, 1024], P('dp')
- o_weight_grad: float32 [1024, 2048], P('dp')
- q_gain_grad: float32 [128], P('dp')
- k_gain_grad: float32 [128], P('dp')
- mlp_gain_grad: float32 [1024], P('dp')
- gate_weight_grad: float32 [1024, 3072], P('dp')
- up_weight_grad: float32 [1024, 3072], P('dp')
- down_weight_grad: float32 [1024, 3072], P('dp')
The draws below stay inside these ranges and needn't reach their ends.
Inputs may be any that keep to these rules, and one draw needn't show every extreme that they name: `segments`: document numbers never fall along the row and rise by one at each new document; every document lies within two consecutive blocks of 512 tokens of the row and starts in the second half of the first of them if it reaches into the next; no document is longer than 512 tokens, and one is exactly that long.
All inputs are finite; a program needn't handle non-finite values.
Results may differ from the reference program's by a relative error of at most 0.015.
Values may be sent and summed in bfloat16 or wider, within the bound.
No kernel may reach another device: no remote copies, remote signals or barrier semaphores. Data moves between devices by JAX's collectives and lax.ppermute only.
A program may use at most 192 MiB of HBM per device.

```python
import math
import jax
import jax.numpy as jnp
from jax import lax

D = 1024
H = 16
KV = 8
HD = 128
FF = 3072
TOK_DEV = 512
TOKENS = 16384


def draw_segments(key, part):
    key = jax.random.fold_in(key, 7)
    block_count = TOKENS // TOK_DEV
    half_rows = TOK_DEV // 2
    first_key, second_key, chosen_key = jax.random.split(key, 3)
    first_cut = jax.random.randint(first_key, (block_count, 1), 1, half_rows)
    second_cut = jax.random.randint(second_key, (block_count, 1), half_rows + 1, TOK_DEV)
    chosen = jax.random.randint(chosen_key, (), 1, block_count)
    block_rows = jnp.arange(block_count, dtype=jnp.int32)[:, None]
    first_cut = jnp.where(block_rows == chosen, half_rows, first_cut)
    second_cut = jnp.where(block_rows == chosen - 1, half_rows, second_cut)
    local_place = jnp.arange(TOK_DEV, dtype=jnp.int32)[None, :]
    numbers = 2 * block_rows + (local_place >= first_cut).astype(jnp.int32) + (local_place >= second_cut).astype(jnp.int32)
    return numbers.reshape(TOKENS).astype(jnp.int32)


def steps_of(stream_key, dims, pieces, smallest, largest):
    gain, own = 1.0, jax.random.fold_in(stream_key, 6)
    for axis_at, parts in pieces:
        draws = jnp.exp(jax.random.uniform(jax.random.fold_in(own, axis_at), (parts,), jnp.float32, smallest / len(pieces), largest / len(pieces)))
        gain = gain * jnp.repeat(draws, dims[axis_at] // parts).reshape([-1 if axis == axis_at else 1 for axis in range(len(dims))])
    return gain


def scatter_about(stream_key, shape, spread, most, shards=(), kind=jnp.bfloat16):
    level = steps_of(stream_key, shape, shards, -0.22, 0.18) if shards else 1.0
    result = jax.random.normal(stream_key, shape, jnp.float32) * spread * level
    return jnp.minimum(jnp.maximum(result, -most), most).astype(kind)


def setup_inputs(seed: int = 0) -> dict:
    key_of = jax.random.split(jax.random.key(seed), 15)
    return {
        "tokens": scatter_about(key_of[0], (TOKENS, D), 1.0, 6.0, ((0, 32),)),
        "segments": draw_segments(jax.random.fold_in(key_of[14], 71), 0),
        "norm_gain": jnp.clip(1.0 + 0.15 * jax.random.normal(key_of[2], (D,), jnp.float32), 0.25, 1.75).astype(jnp.bfloat16),
        "q_weight": scatter_about(key_of[3], (D, H * HD), D ** -0.5, 0.1875, ((0, 32),)),
        "k_weight": scatter_about(key_of[4], (D, KV * HD), D ** -0.5, 0.1875, ((0, 32),)),
        "v_weight": scatter_about(key_of[5], (D, KV * HD), D ** -0.5, 0.1875, ((0, 32),)),
        "o_weight": scatter_about(key_of[6], (D, H * HD), (H * HD * 8 // TOK_DEV) ** -0.5, 1.0, ((0, 32),)),
        "q_gain": jnp.clip(1.0 + 0.15 * jax.random.normal(key_of[7], (HD,), jnp.float32), 0.25, 1.75).astype(jnp.bfloat16),
        "k_gain": jnp.clip(1.0 + 0.15 * jax.random.normal(key_of[8], (HD,), jnp.float32), 0.25, 1.75).astype(jnp.bfloat16),
        "mlp_gain": jnp.clip(1.0 + 0.15 * jax.random.normal(key_of[9], (D,), jnp.float32), 0.25, 1.75).astype(jnp.bfloat16),
        "gate_weight": scatter_about(key_of[10], (D, FF), D ** -0.5, 0.1875, ((0, 32),)),
        "up_weight": scatter_about(key_of[11], (D, FF), D ** -0.5, 0.1875, ((0, 32),)),
        "down_weight": scatter_about(key_of[12], (D, FF), FF ** -0.5, 0.109375, ((0, 32),)),
        "cotangent": scatter_about(key_of[13], (TOKENS, D), 1.0, 6.0, ((0, 32),)),
    }


epsilon = 1e-06
rope_base = 1000000.0

@jax.custom_vjp
def low(v):
    return lax.optimization_barrier(v.astype(jnp.bfloat16)).astype(jnp.float32)

@jax.custom_vjp
def low_back(v):
    return v

def low_keep(v):
    return (low(v), None)

def low_pass(kept, grad):
    return (grad,)

def back_keep(v):
    return (v, None)

def back_low(kept, grad):
    return (low(grad),)
low.defvjp(low_keep, low_pass)
low_back.defvjp(back_keep, back_low)

def inverse_rms(values):
    return lax.rsqrt(lax.optimization_barrier(jnp.mean(values * values, axis=-1, keepdims=True)) + epsilon)

def rotate(values, cosines, sines):
    half_size = values.shape[-1] // 2
    first_half = values[..., :half_size]
    second = values[..., half_size:]
    return jnp.concatenate([first_half * cosines - second * sines, second * cosines + first_half * sines], axis=-1)

def product(left_side, right_side):
    return jnp.dot(left_side, right_side, precision=lax.Precision.HIGHEST, preferred_element_type=jnp.float32)

def product_cols(left_side, right_side):
    return lax.dot_general(left_side, right_side, (((1,), (1,)), ((), ())), precision=lax.Precision.HIGHEST, preferred_element_type=jnp.float32)

def rope_tables(segments):
    position = jnp.arange(TOKENS, dtype=jnp.int32)
    changes = jnp.concatenate([jnp.ones((1,), bool), segments[1:] != segments[:-1]])
    starts = lax.cummax(jnp.where(changes, position, 0), axis=0)
    offsets = (position - starts).astype(jnp.float32)
    frequency = jnp.exp(jnp.arange(HD // 2, dtype=jnp.float32) * (-2.0 * math.log(rope_base) / HD))
    angles = offsets[:, None] * frequency[None, :]
    return (jnp.cos(angles)[:, None, :], jnp.sin(angles)[:, None, :])

def attention(queries, keys_all, values_all, segments):
    block_rows = 2 * TOK_DEV
    block_count = TOKENS // block_rows
    group_count = H // KV
    scales = HD ** (-0.5)
    keys_pad = jnp.concatenate([jnp.zeros((TOK_DEV, KV, HD), jnp.float32), keys_all])
    values_pad = jnp.concatenate([jnp.zeros((TOK_DEV, KV, HD), jnp.float32), values_all])
    segment_pad = jnp.concatenate([jnp.full((TOK_DEV,), -1, jnp.int32), segments])

    def one_block(block_index):
        block_start = block_index * block_rows
        block_query = lax.dynamic_slice_in_dim(queries, block_start, block_rows).reshape(block_rows, KV, group_count, HD)
        block_key = lax.dynamic_slice_in_dim(keys_pad, block_start, block_rows + TOK_DEV)
        block_value = lax.dynamic_slice_in_dim(values_pad, block_start, block_rows + TOK_DEV)
        query_segment = lax.dynamic_slice_in_dim(segments, block_start, block_rows)
        key_segment = lax.dynamic_slice_in_dim(segment_pad, block_start, block_rows + TOK_DEV)
        query_place = block_start + jnp.arange(block_rows, dtype=jnp.int32)
        key_place = block_start - TOK_DEV + jnp.arange(block_rows + TOK_DEV, dtype=jnp.int32)
        raw_scores = low_back(jnp.einsum('qkgd,ckd->kgqc', block_query, block_key, precision=lax.Precision.HIGHEST) * scales)
        visible = (query_segment[:, None] == key_segment[None, :]) & (key_place[None, :] <= query_place[:, None])
        raw_scores = jnp.where(visible[None, None], raw_scores, -1e+30)
        row_max = lax.optimization_barrier(jnp.max(raw_scores, axis=-1, keepdims=True))
        weights = jnp.exp(raw_scores - row_max)
        softmax = low(weights / lax.optimization_barrier(jnp.sum(weights, axis=-1, keepdims=True)))
        mixed_block = jnp.einsum('kgqc,ckd->qkgd', softmax, block_value, precision=lax.Precision.HIGHEST)
        return mixed_block.reshape(block_rows, H * HD)
    blocks = lax.map(jax.checkpoint(one_block), jnp.arange(block_count, dtype=jnp.int32))
    return blocks.reshape(TOKENS, H * HD)

def layer(tokens, norm_gain, q_weight, k_weight, v_weight, o_weight, q_gain, k_gain, mlp_gain, gate_weight, up_weight, down_weight, segments, cosines, sines):
    attn_in = low(tokens * inverse_rms(tokens) * norm_gain)
    query_proj = low_back(product(attn_in, q_weight)).reshape(TOKENS, H, HD)
    key_proj = low_back(product(attn_in, k_weight)).reshape(TOKENS, KV, HD)
    values_all = low(low_back(product(attn_in, v_weight))).reshape(TOKENS, KV, HD)
    queries = low(rotate(query_proj * inverse_rms(query_proj) * q_gain, cosines, sines))
    keys_all = low(rotate(key_proj * inverse_rms(key_proj) * k_gain, cosines, sines))
    attended = low(low_back(attention(queries, keys_all, values_all, segments)))
    hidden_state = tokens + low_back(product_cols(attended, o_weight))
    mlp_in = low(hidden_state * inverse_rms(hidden_state) * mlp_gain)
    gate_proj = low_back(product(mlp_in, gate_weight))
    up_proj = low_back(product(mlp_in, up_weight))
    activated = low(jax.nn.silu(gate_proj) * up_proj)
    return hidden_state + low_back(product_cols(activated, down_weight))

def reference(tokens, segments, norm_gain, q_weight, k_weight, v_weight, o_weight, q_gain, k_gain, mlp_gain, gate_weight, up_weight, down_weight, cotangent):
    primals = tuple((item.astype(jnp.float32) for item in (tokens, norm_gain, q_weight, k_weight, v_weight, o_weight, q_gain, k_gain, mlp_gain, gate_weight, up_weight, down_weight)))
    cosines, sines = rope_tables(segments)

    def forward(*arrays):
        return layer(*arrays, segments, cosines, sines)
    mixed_out, pullback = jax.vjp(forward, *primals)
    grads = pullback(cotangent.astype(jnp.float32))
    return (mixed_out.astype(jnp.bfloat16), grads[0].astype(jnp.bfloat16), grads[1], grads[2], grads[3], grads[4], grads[5], grads[6], grads[7], grads[8], grads[9], grads[10], grads[11])
```

```python
import functools
import math

import jax
import jax.numpy as jnp
from jax import lax
from jax.experimental import pallas as pl
from jax.experimental.pallas import tpu as pltpu
from jax.sharding import PartitionSpec as P

epsilon = 1e-06
rope_base = 1000000.0
low = jnp.bfloat16
full = jnp.float32
vmem_limit = 48 * 1024 * 1024
barrier = lax.optimization_barrier


def dot(left_side, right_side, left_dim=1, right_dim=0, kind=full):
    return lax.dot_general(
        left_side,
        right_side,
        (((left_dim,), (right_dim,)), ((), ())),
        preferred_element_type=kind,
    )


def inverse_rms(values):
    return lax.rsqrt(jnp.mean(values * values, axis=-1, keepdims=True) + epsilon)


def rotate(values, cosines, sines):
    half_size = values.shape[-1] // 2
    first_half = values[..., :half_size]
    second = values[..., half_size:]
    return jnp.concatenate(
        [first_half * cosines - second * sines, second * cosines + first_half * sines], axis=-1
    )


def norm_back(gradient, normed, scales):
    return scales * (gradient - normed * jnp.mean(gradient * normed, axis=-1, keepdims=True))


class Slice:
    def __init__(self):
        self.count = lax.axis_size("dp")
        self.chips = self.count // 2
        self.side = 1
        while 4 * self.side * self.side < self.chips:
            self.side *= 2
        self.device = lax.axis_index("dp")
        self.core = self.device % 2
        self.chip = self.device // 2

    def flip(self, array, mask):
        return lax.ppermute(array, "dp", [(i, i ^ mask) for i in range(self.count)])

    def ring(self, array, by):
        step = 2 * self.side * self.side * by
        return lax.ppermute(
            array, "dp", [(i, (i + step) % self.count) for i in range(self.count)]
        )

    def chip_along(self, array, by):
        pairs = [(i, i + 2 * by) for i in range(self.count) if 0 <= i + 2 * by < self.count]
        return lax.ppermute(array, "dp", pairs)

    def pair(self, array):
        return self.flip(array, 1)

    def by_core(self, mine, other, axis=0):
        return jnp.where(
            self.core == 0,
            jnp.concatenate([mine, other], axis=axis),
            jnp.concatenate([other, mine], axis=axis),
        )

    def halves(self, array, axis=0):
        size = array.shape[axis] // 2
        mine = lax.dynamic_slice_in_dim(array, self.core * size, size, axis)
        other = lax.dynamic_slice_in_dim(array, (1 - self.core) * size, size, axis)
        return mine, other

    def mask_of(self, name, amount):
        return 2 * amount * (1 if name == "x" else self.side)

    def places(self, chip, unit):
        side = self.side
        entry = jnp.arange(self.chips * unit, dtype=jnp.int32)
        inner, block = entry % unit, entry // unit
        along_z, along_x, along_y = block % 4, block // 4 % side, block // (4 * side)
        own_x, own_y, own_z = chip % side, chip // side % side, chip // (side * side)
        source = (
            ((own_z - along_z + 4) % 4) * side * side + (own_y ^ along_y) * side + (own_x ^ along_x)
        )
        return source * unit + inner

    def gather_z(self, block):
        blocks = [block]
        for _ in range(3):
            blocks.append(self.ring(blocks[-1], 1))
        return blocks

    def gather_plane_first(self, block, name):
        return [block] + [
            self.flip(block, self.mask_of(name, m)) for m in range(1, self.side)
        ]

    def gather_plane_second(self, pieces, name):
        side = self.side
        rows = [pieces]
        for m in range(1, side):
            rows.append([self.flip(piece, self.mask_of(name, m)) for piece in pieces])
        if name == "y":
            return [rows[y][x] for y in range(side) for x in range(side)]
        return [rows[x][y] for y in range(side) for x in range(side)]

    def scatter(self, array, first):
        side = self.side
        pieces = jnp.split(array, side * side)
        current = {(y, x): pieces[y * side + x] for y in range(side) for x in range(side)}
        for name in (first, "y" if first == "x" else "x"):
            at = 1 if name == "x" else 0
            kept = {}
            for key in [key for key in current if key[at] == 0]:
                total = current[key].astype(full)
                for m in range(1, side):
                    sent = (key[0], m) if name == "x" else (m, key[1])
                    total = total + self.flip(current[sent], self.mask_of(name, m)).astype(full)
                kept[key] = total.astype(array.dtype)
            current = kept
        blocks = jnp.split(current[(0, 0)], 4)
        total = blocks[0].astype(full)
        for m in range(1, 4):
            total = total + self.ring(blocks[m], -m).astype(full)
        return total

    def finish(self, total):
        mine, other = self.halves(total)
        return self.by_core(mine, self.pair(other), axis=1)


def score_bias(query_segments, key_segments, rows, halo):
    key_count, query_count = key_segments.shape[0], query_segments.shape[1]
    key_place = lax.broadcasted_iota(jnp.int32, (key_count, query_count), 0) - halo
    query_place = lax.broadcasted_iota(jnp.int32, (key_count, query_count), 1)
    seen = (key_segments == query_segments) & (key_place <= query_place)
    return jnp.where(seen, 0.0, -1e30).astype(full)


def parts_of(rows, halo):
    return (((0, halo), 2 * halo), ((halo, rows), halo + rows))


def forward_kernel(scale, rows, halo, q_ref, k_ref, v_ref, qs_ref, ks_ref, out_ref, bias_ref):
    block = pl.program_id(1)
    start = pl.multiple_of(block * rows, rows)
    window = halo + rows
    head_size = k_ref.shape[1]

    @pl.when(pl.program_id(0) == 0)
    def _():
        bias_ref[block] = score_bias(
            qs_ref[...], ks_ref[pl.ds(start, window), :], rows, halo
        )

    for (low_row, high_row), key_count in parts_of(rows, halo):
        keys = k_ref[pl.ds(start, key_count), :]
        values = v_ref[pl.ds(start, key_count), :]
        bias = bias_ref[block, :key_count, low_row:high_row]
        for group in range(q_ref.shape[1] // head_size):
            lanes = slice(group * head_size, (group + 1) * head_size)
            query = q_ref[low_row:high_row, lanes]
            scores = dot(keys, query, 1, 1) * scale + bias
            weights = jnp.exp2(scores)
            total = jnp.sum(weights, axis=0, keepdims=True)
            probs = (weights * (1.0 / total)).astype(low)
            mixed = dot(values, probs, 0, 0)
            out_ref[low_row:high_row, lanes] = mixed.T.astype(low)


def backward_kernel(
    scale, rows, halo, q_ref, k_ref, v_ref, g_ref, qs_ref, ks_ref, dq_ref, dk_ref, dv_ref, bias_ref
):
    block = pl.program_id(1)
    start = pl.multiple_of(block * rows, rows)
    window = halo + rows
    head_size = k_ref.shape[1]
    factor = head_size ** (-0.5)

    @pl.when(pl.program_id(0) == 0)
    def _():
        bias_ref[block] = score_bias(
            qs_ref[...], ks_ref[pl.ds(start, window), :], rows, halo
        )

    @pl.when(block == 0)
    def _():
        dk_ref[...] = jnp.zeros_like(dk_ref)
        dv_ref[...] = jnp.zeros_like(dv_ref)

    for (low_row, high_row), key_count in parts_of(rows, halo):
        keys = k_ref[pl.ds(start, key_count), :]
        values = v_ref[pl.ds(start, key_count), :]
        bias = bias_ref[block, :key_count, low_row:high_row]
        key_sum = None
        value_sum = None
        for group in range(q_ref.shape[1] // head_size):
            lanes = slice(group * head_size, (group + 1) * head_size)
            query = q_ref[low_row:high_row, lanes]
            grad = g_ref[low_row:high_row, lanes]
            weights = jnp.exp2(dot(keys, query, 1, 1) * scale + bias)
            total = jnp.sum(weights, axis=0, keepdims=True)
            softmax = weights * (1.0 / total)
            prob_grad = dot(values, grad, 1, 1)
            product = softmax * prob_grad
            mean = jnp.sum(product, axis=0, keepdims=True)
            score_grad = (product - softmax * mean).astype(low)
            value_term = dot(softmax.astype(low), grad)
            key_term = dot(score_grad, query)
            value_sum = value_term if value_sum is None else value_sum + value_term
            key_sum = key_term if key_sum is None else key_sum + key_term
            dq_ref[low_row:high_row, lanes] = dot(keys, score_grad, 0, 0).T * factor
        dk_ref[pl.ds(start, key_count), :] += key_sum * factor
        dv_ref[pl.ds(start, key_count), :] += value_sum


def attention_specs(rows, halo, token_count, group_lanes, head_size):
    queries = pl.BlockSpec((rows, group_lanes), lambda h, b: (b, h))
    keys = pl.BlockSpec((halo + token_count, head_size), lambda h, b: (0, h))
    query_segments = pl.BlockSpec((1, rows), lambda h, b: (0, b))
    key_segments = pl.BlockSpec((halo + token_count, 1), lambda h, b: (0, 0))
    return queries, keys, query_segments, key_segments


def attention_forward(queries, keys, values, query_segments, key_segments, rows, halo, head_size):
    token_count = queries.shape[0]
    heads = keys.shape[1] // head_size
    q_spec, k_spec, qs_spec, ks_spec = attention_specs(
        rows, halo, token_count, queries.shape[1] // heads, head_size
    )
    scale = head_size ** (-0.5) / math.log(2.0)
    return pl.pallas_call(
        functools.partial(forward_kernel, scale, rows, halo),
        grid=(heads, token_count // rows),
        in_specs=[q_spec, k_spec, k_spec, qs_spec, ks_spec],
        out_specs=q_spec,
        out_shape=jax.ShapeDtypeStruct(queries.shape, low),
        scratch_shapes=[pltpu.VMEM((token_count // rows, halo + rows, rows), full)],
        compiler_params=pltpu.CompilerParams(vmem_limit_bytes=vmem_limit),
        cost_estimate=pl.CostEstimate(
            flops=4 * queries.size * (halo + rows),
            bytes_accessed=2 * (2 * queries.size + 2 * keys.size),
            transcendentals=queries.size // head_size * (halo + rows),
        ),
        name="attention_forward",
    )(queries, keys, values, query_segments, key_segments)


def attention_backward(
    queries, keys, values, grads, query_segments, key_segments, rows, halo, head_size
):
    token_count = queries.shape[0]
    heads = keys.shape[1] // head_size
    q_spec, k_spec, qs_spec, ks_spec = attention_specs(
        rows, halo, token_count, queries.shape[1] // heads, head_size
    )
    scale = head_size ** (-0.5) / math.log(2.0)
    return pl.pallas_call(
        functools.partial(backward_kernel, scale, rows, halo),
        grid=(heads, token_count // rows),
        in_specs=[q_spec, k_spec, k_spec, q_spec, qs_spec, ks_spec],
        out_specs=[q_spec, k_spec, k_spec],
        out_shape=[
            jax.ShapeDtypeStruct(queries.shape, full),
            jax.ShapeDtypeStruct(keys.shape, full),
            jax.ShapeDtypeStruct(keys.shape, full),
        ],
        scratch_shapes=[pltpu.VMEM((token_count // rows, halo + rows, rows), full)],
        compiler_params=pltpu.CompilerParams(vmem_limit_bytes=vmem_limit),
        cost_estimate=pl.CostEstimate(
            flops=10 * queries.size * (halo + rows),
            bytes_accessed=8 * queries.size + 12 * keys.size,
            transcendentals=queries.size // head_size * (halo + rows),
        ),
        name="attention_backward",
    )(queries, keys, values, grads, query_segments, key_segments)


def per_device(
    tokens,
    segments,
    norm_gain,
    q_weight,
    k_weight,
    v_weight,
    o_weight,
    q_gain,
    k_gain,
    mlp_gain,
    gate_weight,
    up_weight,
    down_weight,
    cotangent,
):
    net = Slice()
    row_count, width = tokens.shape
    halo = row_count // 2
    chip_rows = 2 * row_count
    weight_rows = q_weight.shape[0]
    head_size = q_gain.shape[0] * net.count
    gain_rows = q_gain.shape[0]

    def column_block(weight):
        mine, other = net.halves(weight, axis=1)
        return mine, other

    def extra_column(gain):
        return jnp.pad(gain[:, None], ((0, weight_rows - gain.shape[0]), (0, 0)))

    extras = jnp.concatenate(
        [extra_column(gain) for gain in (norm_gain, mlp_gain, q_gain, k_gain)]
        + [jnp.zeros((weight_rows, 124), low)],
        axis=1,
    )
    q_mine, q_other = net.halves(q_weight, 1)
    k_mine, k_other = net.halves(k_weight, 1)
    v_mine, v_other = net.halves(v_weight, 1)
    o_mine, o_other = net.halves(o_weight, 1)
    gate_mine, gate_other = net.halves(gate_weight, 1)
    up_mine, up_other = net.halves(up_weight, 1)
    down_mine, down_other = net.halves(down_weight, 1)

    def chip_block(mine, other):
        return net.by_core(jnp.concatenate(mine, 1), net.pair(jnp.concatenate(other, 1)))

    first_block = chip_block(
        [q_mine, extras, k_mine, v_mine], [q_other, extras, k_other, v_other]
    )
    q_cols = q_mine.shape[1]
    k_cols = k_mine.shape[1]
    o_cols = o_mine.shape[1]
    ff_cols = gate_mine.shape[1]
    rest = [[o_mine], [gate_mine, up_mine], [down_mine]]
    rest_other = [[o_other], [gate_other, up_other], [down_other]]
    blocks = [first_block] + [chip_block(mine, other) for mine, other in zip(rest, rest_other)]
    cuts = [q_cols + 128, o_cols // 2, ff_cols, ff_cols // 2]
    gathered = []
    held_z, held_plane = None, None
    for block, cut in zip(blocks, cuts):
        if held_z is not None:
            block, held_z = barrier((block, held_z))
        left = net.gather_z(block[:, :cut])
        right = net.gather_z(block[:, cut:])
        held_z = (left[-1], right[-1])
        left = jnp.concatenate(left)
        right = jnp.concatenate(right)
        if held_plane is not None:
            left, right, held_plane = barrier((left, right, held_plane))
        left = net.gather_plane_first(left, "y")
        right = net.gather_plane_first(right, "x")
        held_plane = (left[-1], right[-1])
        left = net.gather_plane_second(left, "x")
        right = net.gather_plane_second(right, "y")
        gathered.append((jnp.concatenate(left), jnp.concatenate(right)))
    (q_extra, kv_full), (o_left, o_right), (gate_full, up_full), (down_left, down_right) = gathered
    q_full = q_extra[:, :q_cols]
    gains = q_extra[:, q_cols : q_cols + 4].astype(full)
    o_full = jnp.concatenate([o_left, o_right], 1)
    down_full = jnp.concatenate([down_left, down_right], 1)

    places = net.places(net.chip, 2 * weight_rows)
    order = (jnp.arange(width, dtype=jnp.int32)[:, None] == places[None, :]).astype(low)
    head_places = net.places(net.chip, 2 * gain_rows)
    head_order = (
        jnp.arange(head_size, dtype=jnp.int32)[:, None] == head_places[None, :]
    ).astype(full)

    def head_gain(column):
        spread = column.reshape(net.count, weight_rows)[:, :gain_rows].reshape(1, head_size)
        return jnp.sum(head_order * spread, axis=1)

    gain_one = gains[:, 0]
    gain_two = gains[:, 1]
    q_gain_full = head_gain(gains[:, 2])
    k_gain_full = head_gain(gains[:, 3])

    chip_tokens = net.by_core(tokens, net.pair(tokens))
    before_tokens = net.chip_along(chip_tokens[chip_rows - halo :], 1)
    chip_segments = net.by_core(segments, net.pair(segments))
    before_segments = net.chip_along(chip_segments[chip_rows - halo :], 1)
    before_segments = jnp.where(net.chip > 0, before_segments, -1)
    window_tokens = jnp.concatenate([before_tokens, chip_tokens])
    window_segments = jnp.concatenate([before_segments, chip_segments])
    counter = jnp.arange(halo + chip_rows, dtype=jnp.int32)
    changes = jnp.concatenate([jnp.ones((1,), bool), window_segments[1:] != window_segments[:-1]])
    starts = lax.cummax(jnp.where(changes, counter, 0), axis=0)
    offsets = (counter - starts).astype(full)
    frequency = jnp.exp(
        jnp.arange(head_size // 2, dtype=full) * (-2.0 * math.log(rope_base) / head_size)
    )
    angles = offsets[:, None] * frequency[None, :]
    cosines = jnp.cos(angles)[:, None, :]
    sines = jnp.sin(angles)[:, None, :]
    q_cosines, q_sines = cosines[halo:], sines[halo:]
    query_segments = chip_segments[None, :]
    key_segments = window_segments[:, None]

    ordered = dot(window_tokens, order, kind=low)
    inputs = ordered.astype(full)
    attn_in = (inputs * inverse_rms(inputs) * gain_one).astype(low)
    chip_attn_in = attn_in[halo:]
    own_inputs = lax.dynamic_slice_in_dim(ordered, halo + net.core * row_count, row_count).astype(
        full
    )
    scale_one = inverse_rms(own_inputs)
    normed_one = own_inputs * scale_one
    own_cotangent = dot(cotangent, order, kind=low)
    chip_cotangent = jnp.concatenate([own_cotangent, net.pair(own_cotangent)])

    query_proj = dot(chip_attn_in, q_full).reshape(chip_rows, -1, head_size)
    kv_proj = dot(attn_in, kv_full)
    key_proj = kv_proj[:, :k_cols].reshape(halo + chip_rows, -1, head_size)
    values = kv_proj[:, k_cols:].astype(low)
    query_scale = inverse_rms(query_proj)
    query_normed = query_proj * query_scale
    key_scale = inverse_rms(key_proj)
    key_normed = key_proj * key_scale
    queries = (
        rotate(query_normed * q_gain_full, q_cosines, q_sines).astype(low).reshape(chip_rows, -1)
    )
    keys = (
        rotate(key_normed * k_gain_full, cosines, sines).astype(low).reshape(halo + chip_rows, -1)
    )
    attended = attention_forward(
        queries, keys, values, query_segments, key_segments, row_count, halo, head_size
    )

    attended_mine, attended_other = net.halves(attended)
    branch_sent = net.pair(dot(attended_other, o_full, 1, 1))
    hidden_state = own_inputs + (dot(attended_mine, o_full, 1, 1) + branch_sent)
    scale_two = inverse_rms(hidden_state)
    normed_two = hidden_state * scale_two
    mlp_own = (normed_two * gain_two).astype(low)
    mlp_in = jnp.concatenate([mlp_own, net.pair(mlp_own)])
    gate_proj = dot(mlp_in, gate_full)
    up_proj = dot(mlp_in, up_full)
    sigmoid_gate = jax.nn.sigmoid(gate_proj)
    activated = (gate_proj * sigmoid_gate * up_proj).astype(low)
    down_grad = dot(chip_cotangent, activated, 0, 0, low)
    act_grad = dot(chip_cotangent, down_full)
    gate_grad = (
        act_grad * up_proj * sigmoid_gate * (1.0 + gate_proj * (1.0 - sigmoid_gate))
    ).astype(low)
    up_grad = (act_grad * gate_proj * sigmoid_gate).astype(low)
    mlp_grad_sent = net.pair(
        dot(gate_grad[row_count:], gate_full, 1, 1) + dot(up_grad[row_count:], up_full, 1, 1)
    )
    mlp_in_grad = (
        dot(gate_grad[:row_count], gate_full, 1, 1)
        + dot(up_grad[:row_count], up_full, 1, 1)
        + mlp_grad_sent
    )
    gate_w_grad = dot(mlp_in, gate_grad, 0, 0, low)
    up_w_grad = dot(mlp_in, up_grad, 0, 0, low)
    out_sent = net.pair(dot(activated[row_count:], down_full, 1, 1))
    mixed_out = (
        hidden_state + (dot(activated[:row_count], down_full, 1, 1) + out_sent)
    ).astype(low)
    mixed_out = dot(mixed_out, order, 1, 1, low)

    gain_two_grad = jnp.sum(mlp_in_grad * normed_two, axis=0)
    hidden_grad = own_cotangent.astype(full) + norm_back(
        mlp_in_grad * gain_two, normed_two, scale_two
    )
    branch_own = hidden_grad.astype(low)
    branch_low = net.by_core(branch_own, net.pair(branch_own))
    attended_grad = dot(branch_low, o_full, kind=low)
    o_w_grad = dot(branch_low, attended, 0, 0, low)
    query_grad, key_grad, value_grad = attention_backward(
        queries,
        keys,
        values,
        attended_grad,
        query_segments,
        key_segments,
        row_count,
        halo,
        head_size,
    )
    query_back = rotate(query_grad.reshape(query_proj.shape), q_cosines, -q_sines)
    key_back = rotate(key_grad.reshape(key_proj.shape), cosines, -sines)
    q_gain_grad = jnp.sum(query_back * query_normed, axis=(0, 1))
    k_gain_grad = jnp.sum(key_back * key_normed, axis=(0, 1))
    query_low = (
        norm_back(query_back * q_gain_full, query_normed, query_scale)
        .astype(low)
        .reshape(chip_rows, -1)
    )
    key_low = (
        norm_back(key_back * k_gain_full, key_normed, key_scale)
        .astype(low)
        .reshape(halo + chip_rows, -1)
    )
    value_low = value_grad.astype(low)
    kv_low = jnp.concatenate([key_low, value_low], axis=1)
    q_w_grad = dot(chip_attn_in, query_low, 0, 0, low)
    kv_w_grad = dot(attn_in, kv_low, 0, 0, low)

    before_grad = net.chip_along(dot(kv_low[:halo], kv_full, 1, 1, low), -1)
    next_places = net.places(net.chip + 1, 2 * weight_rows)
    next_order = (next_places[:, None] == places[None, :]).astype(low)
    before_grad = dot(before_grad, next_order)
    chip_grad = dot(query_low, q_full, 1, 1) + dot(kv_low[halo:], kv_full, 1, 1)
    chip_grad = jnp.concatenate(
        [chip_grad[: chip_rows - halo], chip_grad[chip_rows - halo :] + before_grad]
    )
    grad_mine, grad_other = net.halves(chip_grad)
    attn_in_grad = grad_mine + net.pair(grad_other)
    gain_one_grad = jnp.sum(attn_in_grad * normed_one, axis=0)
    input_grad = (hidden_grad + norm_back(attn_in_grad * gain_one, normed_one, scale_one)).astype(
        low
    )
    input_grad = dot(input_grad, order, 1, 1, low)

    down_cut = ff_cols // 2
    o_cut = o_cols // 2
    down_sum = jnp.concatenate(
        [net.scatter(down_grad[:, :down_cut], "x"), net.scatter(down_grad[:, down_cut:], "y")], 1
    )
    gate_sum = net.scatter(gate_w_grad, "x")
    up_sum = net.scatter(up_w_grad, "y")
    o_sum = jnp.concatenate(
        [net.scatter(o_w_grad[:, :o_cut], "x"), net.scatter(o_w_grad[:, o_cut:], "y")], 1
    )
    q_sum = net.scatter(q_w_grad, "x")
    kv_sum = net.scatter(kv_w_grad, "y")

    def head_sum(gradient):
        return jnp.sum(head_order * gradient[:, None], axis=0).reshape(net.chips, 2, gain_rows)

    gain_sum = jnp.concatenate(
        [
            gain_one_grad.reshape(net.chips, 2, weight_rows),
            gain_two_grad.reshape(net.chips, 2, weight_rows),
            head_sum(q_gain_grad),
            head_sum(k_gain_grad),
        ],
        axis=2,
    )
    gain_sum = net.scatter(gain_sum, "x").reshape(2, -1)
    gain_mine, gain_other = net.halves(gain_sum)
    gain_sum = (gain_mine + net.pair(gain_other))[0]
    return (
        mixed_out,
        input_grad,
        gain_sum[:weight_rows],
        net.finish(q_sum),
        net.finish(kv_sum[:, :k_cols]),
        net.finish(kv_sum[:, k_cols:]),
        net.finish(o_sum),
        gain_sum[2 * weight_rows : 2 * weight_rows + gain_rows],
        gain_sum[2 * weight_rows + gain_rows :],
        gain_sum[weight_rows : 2 * weight_rows],
        net.finish(gate_sum),
        net.finish(up_sum),
        net.finish(down_sum),
    )


def solution(mesh):
    rows = P("dp", None)
    line = P("dp")
    return jax.shard_map(
        per_device,
        mesh=mesh,
        in_specs=(
            rows, line, line, rows, rows, rows, rows, line, line, line, rows, rows, rows, rows,
        ),
        out_specs=(
            rows, rows, line, rows, rows, rows, rows, line, line, line, rows, rows, rows,
        ),
        check_vma=False,
    )
```

```python
import functools
import math

import jax
import jax.numpy as jnp
from jax import lax
from jax.experimental import pallas as pl
from jax.experimental.pallas import tpu as pltpu
from jax.sharding import PartitionSpec as P

epsilon = 1e-06
rope_base = 1000000.0
low = jnp.bfloat16
full = jnp.float32
vmem_limit = 48 * 1024 * 1024
barrier = lax.optimization_barrier


def dot(left_side, right_side, left_dim=1, right_dim=0, kind=full):
    return lax.dot_general(
        left_side,
        right_side,
        (((left_dim,), (right_dim,)), ((), ())),
        preferred_element_type=kind,
    )


def inverse_rms(values):
    return lax.rsqrt(jnp.mean(values * values, axis=-1, keepdims=True) + epsilon)


def rotate(values, cosines, sines):
    half_size = values.shape[-1] // 2
    first_half = values[..., :half_size]
    second = values[..., half_size:]
    return jnp.concatenate(
        [first_half * cosines - second * sines, second * cosines + first_half * sines], axis=-1
    )


def norm_back(gradient, normed, scales):
    return scales * (gradient - normed * jnp.mean(gradient * normed, axis=-1, keepdims=True))


class Slice:
    def __init__(self):
        self.count = lax.axis_size("dp")
        self.chips = self.count // 2
        self.side = 1
        while 4 * self.side * self.side < self.chips:
            self.side *= 2
        self.device = lax.axis_index("dp")
        self.core = self.device % 2
        self.chip = self.device // 2

    def flip(self, array, mask):
        return lax.ppermute(array, "dp", [(i, i ^ mask) for i in range(self.count)])

    def ring(self, array, by):
        step = 2 * self.side * self.side * by
        return lax.ppermute(
            array, "dp", [(i, (i + step) % self.count) for i in range(self.count)]
        )

    def chip_along(self, array, by):
        pairs = [(i, i + 2 * by) for i in range(self.count) if 0 <= i + 2 * by < self.count]
        return lax.ppermute(array, "dp", pairs)

    def pair(self, array):
        return self.flip(array, 1)

    def by_core(self, mine, other, axis=0):
        return jnp.where(
            self.core == 0,
            jnp.concatenate([mine, other], axis=axis),
            jnp.concatenate([other, mine], axis=axis),
        )

    def halves(self, array, axis=0):
        size = array.shape[axis] // 2
        mine = lax.dynamic_slice_in_dim(array, self.core * size, size, axis)
        other = lax.dynamic_slice_in_dim(array, (1 - self.core) * size, size, axis)
        return mine, other

    def mask_of(self, name, amount):
        return 2 * amount * (1 if name == "x" else self.side)

    def places(self, chip, unit):
        side = self.side
        entry = jnp.arange(self.chips * unit, dtype=jnp.int32)
        inner, block = entry % unit, entry // unit
        along_z, along_x, along_y = block % 4, block // 4 % side, block // (4 * side)
        own_x, own_y, own_z = chip % side, chip // side % side, chip // (side * side)
        source = (
            ((own_z - along_z + 4) % 4) * side * side + (own_y ^ along_y) * side + (own_x ^ along_x)
        )
        return source * unit + inner

    def gather_z(self, block, steps=3):
        blocks = [block]
        for _ in range(steps):
            blocks.append(self.ring(blocks[-1], 1))
        return blocks

    def plane_first(self, block, name):
        return [block] + [self.flip(block, self.mask_of(name, m)) for m in range(1, self.side)]

    def plane_second(self, pieces, name):
        side = self.side
        rows = [pieces]
        for m in range(1, side):
            rows.append([self.flip(piece, self.mask_of(name, m)) for piece in pieces])
        if name == "y":
            return [rows[y][x] for y in range(side) for x in range(side)]
        return [rows[x][y] for y in range(side) for x in range(side)]

    def quarters(self, pieces):
        each = len(pieces) // 4
        if each == 1:
            return pieces
        return [jnp.concatenate(pieces[at * each : (at + 1) * each]) for at in range(4)]

    def pieces(self, array):
        side = self.side
        parts = jnp.split(array, side * side)
        return {(y, x): parts[y * side + x] for y in range(side) for x in range(side)}

    def scatter_send(self, current, name):
        at = 1 if name == "x" else 0
        brought = {}
        for key in [key for key in current if key[at] == 0]:
            sent = [(key[0], m) if name == "x" else (m, key[1]) for m in range(1, self.side)]
            brought[key] = [
                self.flip(current[other], self.mask_of(name, m + 1))
                for m, other in enumerate(sent)
            ]
        return brought

    def scatter_add(self, current, brought):
        return {
            key: sum([term.astype(full) for term in terms], current[key].astype(full)).astype(
                current[key].dtype
            )
            for key, terms in brought.items()
        }

    def scatter_ring(self, blocks, step):
        return self.ring(blocks[3 - step], -1)

    def scatter_z(self, block):
        blocks = jnp.split(block, 4)
        return [blocks[0]] + [self.ring(blocks[m], -m) for m in range(1, 4)]

    def finish(self, total):
        mine, other = self.halves(total)
        return self.by_core(mine, self.pair(other), axis=1)


def score_bias(query_segments, key_segments, rows, halo):
    key_count, query_count = key_segments.shape[0], query_segments.shape[1]
    key_place = lax.broadcasted_iota(jnp.int32, (key_count, query_count), 0) - halo
    query_place = lax.broadcasted_iota(jnp.int32, (key_count, query_count), 1)
    seen = (key_segments == query_segments) & (key_place <= query_place)
    return jnp.where(seen, 0.0, -1e30).astype(full)


def parts_of(rows, halo):
    return (((0, halo), 2 * halo), ((halo, rows), halo + rows))


def spread(refs, columns=slice(None)):
    return jnp.concatenate([ref[:, columns] for ref in refs], axis=0)


def reorder(refs, quarter, unit):
    size = refs[0].shape[0] // 4
    return jnp.concatenate(
        [
            ref[row : row + unit, :]
            for row in range(quarter * size, (quarter + 1) * size, unit)
            for ref in refs
        ],
        axis=0,
    )


def turn(values, cosines, sines):
    return values * cosines + pltpu.roll(values, values.shape[1] // 2, 1) * sines


def row_rms(values):
    return lax.rsqrt(jnp.mean(values * values, axis=1, keepdims=True) + epsilon)


def call(kernel, name, grid, ins, outs, flops, bytes_accessed, scratch=(), transcendentals=0):
    return pl.pallas_call(
        kernel,
        grid=grid,
        in_specs=[pl.BlockSpec(block, index) for _, block, index in ins],
        out_specs=[pl.BlockSpec(block, index) for _, _, block, index in outs],
        out_shape=[jax.ShapeDtypeStruct(shape, kind) for shape, kind, _, _ in outs],
        scratch_shapes=list(scratch),
        compiler_params=pltpu.CompilerParams(vmem_limit_bytes=vmem_limit),
        cost_estimate=pl.CostEstimate(
            flops=flops, bytes_accessed=bytes_accessed, transcendentals=transcendentals
        ),
        name=name,
    )(*[array for array, _, _ in ins])


def whole_block(array):
    return (array, array.shape, lambda *at: (0,) * array.ndim)


def project_kernel(q_cols, k_cols, x_ref, cos_ref, sin_ref, pick_ref, *refs):
    q_refs, kv_refs = refs[:4], refs[4:8]
    in_ref, q_ref, k_ref, v_ref, qp_ref, kp_ref, rows_ref, heads_ref = refs[8:]
    size = q_refs[0].shape[0]
    head_size = heads_ref.shape[1]
    step = pl.program_id(0)

    @pl.when(step == 0)
    def _():
        heads = jnp.zeros(heads_ref.shape, full)
        for at, ref in enumerate(q_refs):
            rows = ref[:, q_cols : q_cols + 128].astype(full).T[:8]
            rows_ref[:, at * size : (at + 1) * size] = rows
            heads = heads + dot(rows.astype(low), pick_ref[at * size : (at + 1) * size, :])
        heads_ref[...] = heads

    x = x_ref[...].astype(full)
    attn_in = (x * row_rms(x) * rows_ref[0:1, :]).astype(low)
    in_ref[...] = attn_in
    cosines, sines = cos_ref[...], sin_ref[...]

    def product(weights, columns):
        total = None
        for at, ref in enumerate(weights):
            term = dot(attn_in[:, at * size : (at + 1) * size], ref[:, columns])
            total = term if total is None else total + term
        return total

    def heads_of(projected, gain, proj_ref, out_ref, start):
        proj_ref[:, start : start + projected.shape[1]] = projected.astype(low)
        for column in range(0, projected.shape[1], head_size):
            head = projected[:, column : column + head_size]
            head = turn(head * row_rms(head) * gain, cosines, sines)
            out_ref[:, start + column : start + column + head_size] = head.astype(low)

    heads_of(product(kv_refs, slice(0, k_cols)), heads_ref[3:4, :], kp_ref, k_ref, 0)
    v_ref[...] = product(kv_refs, slice(k_cols, None)).astype(low)

    @pl.when(step > 0)
    def _():
        for start in range(0, q_cols, 512):
            heads_of(
                product(q_refs, slice(start, start + 512)), heads_ref[2:3, :], qp_ref, q_ref, start
            )


def project(ordered, cosines, sines, pick, q_parts, kv_parts, q_cols, k_cols, halo):
    row_count, width = ordered.shape
    own = row_count - halo
    head_size = cosines.shape[1]
    tile = lambda i: (i, 0)
    later = lambda i: (jnp.maximum(i - 1, 0), 0)
    fixed = lambda i: (0, 0)
    return call(
        functools.partial(project_kernel, q_cols, k_cols),
        "project",
        (row_count // halo,),
        [
            (ordered, (halo, width), tile),
            (cosines, (halo, head_size), tile),
            (sines, (halo, head_size), tile),
            whole_block(pick),
        ]
        + [whole_block(part) for part in q_parts + kv_parts],
        [
            ((row_count, width), low, (halo, width), tile),
            ((own, q_cols), low, (halo, q_cols), later),
            ((row_count, k_cols), low, (halo, k_cols), tile),
            ((row_count, k_cols), low, (halo, k_cols), tile),
            ((own, q_cols), low, (halo, q_cols), later),
            ((row_count, k_cols), low, (halo, k_cols), tile),
            ((8, width), full, (8, width), fixed),
            ((8, head_size), full, (8, head_size), fixed),
        ],
        2 * row_count * width * (q_cols + 2 * k_cols),
        20 << 20,
    )


def gate_kernel(xm_ref, xo_ref, *refs):
    gate_refs, up_refs = refs[:4], refs[4:8]
    act_ref, to_gate_ref, to_up_ref = refs[8:]
    gate_weight, up_weight = spread(gate_refs), spread(up_refs)
    half = xm_ref.shape[0]
    for at, ref in enumerate((xm_ref, xo_ref)):
        rows = slice(at * half, (at + 1) * half)
        gate = dot(ref[...], gate_weight)
        up = dot(ref[...], up_weight)
        sigma = 1.0 / (1.0 + jnp.exp(-gate))
        silu = gate * sigma
        act_ref[rows, :] = (silu * up).astype(low)
        to_gate_ref[rows, :] = (up * sigma * (1.0 + gate * (1.0 - sigma))).astype(low)
        to_up_ref[rows, :] = silu.astype(low)


def gate_forward(mine, other, gate_parts, up_parts, tile=256):
    half, width = mine.shape
    columns = gate_parts[0].shape[1]
    wide = lambda j: (0, j)
    return call(
        gate_kernel,
        "gate_forward",
        (columns // tile,),
        [whole_block(mine), whole_block(other)]
        + [(part, (part.shape[0], tile), wide) for part in gate_parts + up_parts],
        [((2 * half, columns), low, (2 * half, tile), wide)] * 3,
        8 * half * width * columns,
        16 << 20,
        transcendentals=2 * half * columns,
    )


def mlp_back_kernel(unit, gm_ref, go_ref, to_gate_ref, to_up_ref, *refs):
    down_refs, gate_refs, up_refs = refs[:4], refs[4:8], refs[8:12]
    gate_out, up_out, mine_out, other_out = refs[12:]
    half = gm_ref.shape[0]
    size = gate_refs[0].shape[0]
    down = jnp.concatenate([reorder(down_refs, at, unit) for at in range(4)], axis=0)

    @pl.when(pl.program_id(0) == 0)
    def _():
        mine_out[...] = jnp.zeros_like(mine_out)
        other_out[...] = jnp.zeros_like(other_out)

    for at, (ref, out) in enumerate(((gm_ref, mine_out), (go_ref, other_out))):
        rows = slice(at * half, (at + 1) * half)
        act_grad = dot(ref[...], down)
        gate_grad = (act_grad * to_gate_ref[rows, :].astype(full)).astype(low)
        up_grad = (act_grad * to_up_ref[rows, :].astype(full)).astype(low)
        gate_out[rows, :] = gate_grad
        up_out[rows, :] = up_grad
        for at, (gate_ref, up_ref) in enumerate(zip(gate_refs, up_refs)):
            out[:, at * size : (at + 1) * size] += dot(gate_grad, gate_ref[...], 1, 1) + dot(
                up_grad, up_ref[...], 1, 1
            )


def mlp_backward(
    mine, other, to_gate, to_up, down_parts, gate_parts, up_parts, unit, tile=256
):
    half, width = mine.shape
    columns = to_gate.shape[1]
    wide = lambda j: (0, j)
    fixed = lambda j: (0, 0)
    return call(
        functools.partial(mlp_back_kernel, unit),
        "mlp_backward",
        (columns // tile,),
        [whole_block(mine), whole_block(other)]
        + [(factor, (2 * half, tile), wide) for factor in (to_gate, to_up)]
        + [(part, (part.shape[0], tile), wide) for part in down_parts + gate_parts + up_parts],
        [((2 * half, columns), low, (2 * half, tile), wide)] * 2
        + [((half, width), full, (half, width), fixed)] * 2,
        12 * half * width * columns,
        30 << 20,
    )


def down_kernel(unit, act_ref, *refs):
    down_refs, out_ref = refs[:4], refs[4]
    size = down_refs[0].shape[0]
    for at in range(4):
        out_ref[:, at * size : (at + 1) * size] = dot(
            act_ref[...], reorder(down_refs, at, unit), 1, 1
        )


def down_forward(activated, start, parts, unit, rows, tile=256):
    columns = activated.shape[1]
    width = 4 * parts[0].shape[0]
    first = start // tile
    return call(
        functools.partial(down_kernel, unit),
        "down_forward",
        (rows // tile,),
        [(activated, (tile, columns), lambda i: (i + first, 0))]
        + [whole_block(part) for part in parts],
        [((rows, width), full, (tile, width), lambda i: (i, 0))],
        2 * rows * columns * width,
        8 << 20,
    )[0]


def mix_kernel(core_ref, att_ref, *refs):
    left_refs, right_refs, out_ref = refs[:4], refs[4:8], refs[8]
    size, cut = left_refs[0].shape
    for at, (left, right) in enumerate(zip(left_refs, right_refs)):
        out_ref[:, at * size : (at + 1) * size] = dot(att_ref[:, :cut], left[...], 1, 1) + dot(
            att_ref[:, cut:], right[...], 1, 1
        )


def mix_forward(which, attended, left, right, tile=256):
    rows, columns = attended.shape[0] // 2, attended.shape[1]
    width = 4 * left[0].shape[0]
    steps = rows // tile
    fixed = lambda i, core: (0, 0)
    return pl.pallas_call(
        mix_kernel,
        grid_spec=pltpu.PrefetchScalarGridSpec(
            num_scalar_prefetch=1,
            grid=(steps,),
            in_specs=[pl.BlockSpec((tile, columns), lambda i, core: (core[0] * steps + i, 0))]
            + [pl.BlockSpec(part.shape, fixed) for part in left + right],
            out_specs=pl.BlockSpec((tile, width), lambda i, core: (i, 0)),
        ),
        out_shape=jax.ShapeDtypeStruct((rows, width), full),
        compiler_params=pltpu.CompilerParams(vmem_limit_bytes=vmem_limit),
        cost_estimate=pl.CostEstimate(
            flops=2 * rows * columns * width, bytes_accessed=6 << 20, transcendentals=0
        ),
        name="mix_forward",
    )(which, attended, *left, *right)


def mix_back_kernel(branch_ref, *refs):
    left_refs, right_refs, out_ref = refs[:4], refs[4:8], refs[8]
    size, cut = left_refs[0].shape
    for columns, weights in ((slice(0, cut), left_refs), (slice(cut, None), right_refs)):
        out_ref[:, columns] = dot(branch_ref[...], spread(weights)).astype(low)


def mix_backward(branch, left, right, tile=256):
    rows, width = branch.shape
    columns = left[0].shape[1] + right[0].shape[1]
    rows_of = lambda i: (i, 0)
    return call(
        mix_back_kernel,
        "mix_backward",
        (rows // tile,),
        [(branch, (tile, width), rows_of)] + [whole_block(part) for part in left + right],
        [((rows, columns), low, (tile, columns), rows_of)],
        2 * rows * columns * width,
        6 << 20,
    )[0]


def forward_kernel(scale, rows, halo, q_ref, k_ref, v_ref, qs_ref, ks_ref, out_ref, bias_ref):
    block = pl.program_id(1)
    start = pl.multiple_of(block * rows, rows)
    window = halo + rows
    head_size = k_ref.shape[1]

    @pl.when(pl.program_id(0) == 0)
    def _():
        bias_ref[block] = score_bias(
            qs_ref[...], ks_ref[pl.ds(start, window), :], rows, halo
        )

    for (low_row, high_row), key_count in parts_of(rows, halo):
        keys = k_ref[pl.ds(start, key_count), :]
        values = v_ref[pl.ds(start, key_count), :]
        bias = bias_ref[block, :key_count, low_row:high_row]
        for group in range(q_ref.shape[1] // head_size):
            lanes = slice(group * head_size, (group + 1) * head_size)
            query = q_ref[low_row:high_row, lanes]
            scores = dot(keys, query, 1, 1) * scale + bias
            weights = jnp.exp2(scores)
            total = jnp.sum(weights, axis=0, keepdims=True)
            probs = (weights * (1.0 / total)).astype(low)
            mixed = dot(values, probs, 0, 0)
            out_ref[low_row:high_row, lanes] = mixed.T.astype(low)


def head_back(gradient, projected, gain, cosines, sines):
    scales = row_rms(projected)
    normed = projected * scales
    back = turn(gradient, cosines, -sines)
    gain_grad = jnp.sum(back * normed, axis=0, keepdims=True)
    back = back * gain
    mean = jnp.mean(back * normed, axis=1, keepdims=True)
    return scales * (back - normed * mean), gain_grad


def backward_kernel(
    scale, rows, halo, *refs
):
    q_ref, k_ref, v_ref, g_ref, qp_ref, kp_ref, cos_ref, sin_ref, heads_ref, qs_ref, ks_ref = refs[
        :11
    ]
    dq_ref, dk_ref, dv_ref, gains_ref, bias_ref, key_ref, value_ref = refs[11:]
    head = pl.program_id(0)
    block = pl.program_id(1)
    start = pl.multiple_of(block * rows, rows)
    window = halo + rows
    head_size = k_ref.shape[1]
    factor = head_size ** (-0.5)

    @pl.when(head == 0)
    def _():
        bias_ref[block] = score_bias(
            qs_ref[...], ks_ref[pl.ds(start, window), :], rows, halo
        )

    @pl.when((head == 0) & (block == 0))
    def _():
        gains_ref[...] = jnp.zeros_like(gains_ref)

    @pl.when(block == 0)
    def _():
        key_ref[...] = jnp.zeros_like(key_ref)
        value_ref[...] = jnp.zeros_like(value_ref)

    for (low_row, high_row), key_count in parts_of(rows, halo):
        keys = k_ref[pl.ds(start, key_count), :]
        values = v_ref[pl.ds(start, key_count), :]
        bias = bias_ref[block, :key_count, low_row:high_row]
        here = pl.ds(start + (halo + low_row), high_row - low_row)
        cosines, sines = cos_ref[here, :], sin_ref[here, :]
        key_sum = None
        value_sum = None
        for group in range(q_ref.shape[1] // head_size):
            lanes = slice(group * head_size, (group + 1) * head_size)
            query = q_ref[low_row:high_row, lanes]
            grad = g_ref[low_row:high_row, lanes]
            weights = jnp.exp2(dot(keys, query, 1, 1) * scale + bias)
            total = jnp.sum(weights, axis=0, keepdims=True)
            softmax = weights * (1.0 / total)
            prob_grad = dot(values, grad, 1, 1)
            product = softmax * prob_grad
            mean = jnp.sum(product, axis=0, keepdims=True)
            score_grad = (product - softmax * mean).astype(low)
            value_term = dot(softmax.astype(low), grad)
            key_term = dot(score_grad, query)
            value_sum = value_term if value_sum is None else value_sum + value_term
            key_sum = key_term if key_sum is None else key_sum + key_term
            query_grad = dot(keys, score_grad, 0, 0).T * factor
            query_grad, gain_grad = head_back(
                query_grad,
                qp_ref[low_row:high_row, lanes].astype(full),
                heads_ref[2:3, :],
                cosines,
                sines,
            )
            dq_ref[low_row:high_row, lanes] = query_grad.astype(low)
            gains_ref[0:1, :] += gain_grad
        key_ref[pl.ds(start, key_count), :] += key_sum * factor
        value_ref[pl.ds(start, key_count), :] += value_sum

    @pl.when(block == pl.num_programs(1) - 1)
    def _():
        dv_ref[...] = value_ref[...].astype(low)
        for row in range(0, k_ref.shape[0], halo):
            here = slice(row, row + halo)
            key_grad, gain_grad = head_back(
                key_ref[here, :],
                kp_ref[here, :].astype(full),
                heads_ref[3:4, :],
                cos_ref[here, :],
                sin_ref[here, :],
            )
            dk_ref[here, :] = key_grad.astype(low)
            gains_ref[1:2, :] += gain_grad


def attention_specs(rows, halo, token_count, group_lanes, head_size):
    queries = pl.BlockSpec((rows, group_lanes), lambda h, b: (b, h))
    keys = pl.BlockSpec((halo + token_count, head_size), lambda h, b: (0, h))
    query_segments = pl.BlockSpec((1, rows), lambda h, b: (0, b))
    key_segments = pl.BlockSpec((halo + token_count, 1), lambda h, b: (0, 0))
    return queries, keys, query_segments, key_segments


def attention_forward(queries, keys, values, query_segments, key_segments, rows, halo, head_size):
    token_count = queries.shape[0]
    heads = keys.shape[1] // head_size
    q_spec, k_spec, qs_spec, ks_spec = attention_specs(
        rows, halo, token_count, queries.shape[1] // heads, head_size
    )
    scale = head_size ** (-0.5) / math.log(2.0)
    return pl.pallas_call(
        functools.partial(forward_kernel, scale, rows, halo),
        grid=(heads, token_count // rows),
        in_specs=[q_spec, k_spec, k_spec, qs_spec, ks_spec],
        out_specs=q_spec,
        out_shape=jax.ShapeDtypeStruct(queries.shape, low),
        scratch_shapes=[pltpu.VMEM((token_count // rows, halo + rows, rows), full)],
        compiler_params=pltpu.CompilerParams(vmem_limit_bytes=vmem_limit),
        cost_estimate=pl.CostEstimate(
            flops=4 * queries.size * (halo + rows),
            bytes_accessed=2 * (2 * queries.size + 2 * keys.size),
            transcendentals=queries.size // head_size * (halo + rows),
        ),
        name="attention_forward",
    )(queries, keys, values, query_segments, key_segments)


def attention_backward(
    queries, keys, values, grads, query_proj, key_proj, cosines, sines, heads_gain,
    query_segments, key_segments, rows, halo, head_size,
):
    token_count = queries.shape[0]
    heads = keys.shape[1] // head_size
    lanes = queries.shape[1] // heads
    window = halo + token_count
    scale = head_size ** (-0.5) / math.log(2.0)
    q_at, k_at, fixed = lambda h, b: (b, h), lambda h, b: (0, h), lambda h, b: (0, 0)
    return call(
        functools.partial(backward_kernel, scale, rows, halo),
        "attention_backward",
        (heads, token_count // rows),
        [
            (queries, (rows, lanes), q_at),
            (keys, (window, head_size), k_at),
            (values, (window, head_size), k_at),
            (grads, (rows, lanes), q_at),
            (query_proj, (rows, lanes), q_at),
            (key_proj, (window, head_size), k_at),
            whole_block(cosines),
            whole_block(sines),
            whole_block(heads_gain),
            (query_segments, (1, rows), lambda h, b: (0, b)),
            whole_block(key_segments),
        ],
        [
            (queries.shape, low, (rows, lanes), q_at),
            (keys.shape, low, (window, head_size), k_at),
            (keys.shape, low, (window, head_size), k_at),
            ((8, head_size), full, (8, head_size), fixed),
        ],
        10 * queries.size * (halo + rows),
        24 << 20,
        scratch=[
            pltpu.VMEM((token_count // rows, halo + rows, rows), full),
            pltpu.VMEM((window, head_size), full),
            pltpu.VMEM((window, head_size), full),
        ],
        transcendentals=queries.size // head_size * (halo + rows),
    )


def per_device(
    tokens,
    segments,
    norm_gain,
    q_weight,
    k_weight,
    v_weight,
    o_weight,
    q_gain,
    k_gain,
    mlp_gain,
    gate_weight,
    up_weight,
    down_weight,
    cotangent,
):
    net = Slice()
    row_count, width = tokens.shape
    halo = row_count // 2
    chip_rows = 2 * row_count
    weight_rows = q_weight.shape[0]
    head_size = q_gain.shape[0] * net.count
    gain_rows = q_gain.shape[0]

    q_cols, k_cols, o_cols, ff_cols = (
        weight.shape[1] // 2 for weight in (q_weight, k_weight, o_weight, gate_weight)
    )
    o_cut, ff_cut = o_cols // 2, ff_cols // 2

    column = lax.broadcasted_iota(jnp.int32, (weight_rows, 128), 1)
    extras = jnp.zeros((weight_rows, 128), low)
    for at, gain in enumerate((norm_gain, mlp_gain, q_gain, k_gain)):
        gain = jnp.pad(gain, (0, weight_rows - gain.shape[0]))
        extras = jnp.where(column == at, gain[:, None], extras)

    def chip_block(weights, extra=()):
        split = [net.halves(weight, 1) for weight in weights]
        mine = jnp.concatenate([part[0] for part in split[:1]] + list(extra) + [part[0] for part in split[1:]], 1)
        other = jnp.concatenate([part[1] for part in split[:1]] + list(extra) + [part[1] for part in split[1:]], 1)
        return net.by_core(mine, net.pair(other))

    block_qkv = chip_block([q_weight, k_weight, v_weight], [extras])
    (
        block_qkv, tokens, segments, cotangent, o_weight, gate_weight, up_weight, down_weight
    ) = barrier(
        (block_qkv, tokens, segments, cotangent, o_weight, gate_weight, up_weight, down_weight)
    )
    block_down = chip_block([down_weight])
    block_o = chip_block([o_weight])
    block_mlp = chip_block([gate_weight, up_weight])

    numbers = jnp.broadcast_to(segments.astype(low)[:, None], (row_count, 128))
    both = jnp.concatenate([tokens, numbers], 1)
    both = net.by_core(both, net.pair(both))
    before = net.chip_along(both[chip_rows - halo :], 1)
    chip_tokens, before_tokens = both[:, :width], before[:, :width]
    chip_segments = both[:, width].astype(jnp.int32)
    before_segments = jnp.where(net.chip > 0, before[:, width].astype(jnp.int32), -1)
    window_tokens = jnp.concatenate([before_tokens, chip_tokens])
    window_segments = jnp.concatenate([before_segments, chip_segments])
    counter = jnp.arange(halo + chip_rows, dtype=jnp.int32)
    changes = jnp.concatenate([jnp.ones((1,), bool), window_segments[1:] != window_segments[:-1]])
    starts = lax.cummax(jnp.where(changes, counter, 0), axis=0)
    offsets = (counter - starts).astype(full)
    frequency = jnp.exp(
        (jnp.arange(head_size, dtype=jnp.int32) % (head_size // 2)).astype(full)
        * (-2.0 * math.log(rope_base) / head_size)
    )
    angles = offsets[:, None] * frequency[None, :]
    cosines = jnp.cos(angles)
    sines = jnp.sin(angles) * jnp.where(jnp.arange(head_size) < head_size // 2, -1.0, 1.0)
    query_segments = chip_segments[None, :]
    key_segments = window_segments[:, None]
    places = net.places(net.chip, 2 * weight_rows)
    order = (jnp.arange(width, dtype=jnp.int32)[:, None] == places[None, :]).astype(low)
    head_places = net.places(net.chip, 2 * gain_rows)
    head_order = (
        jnp.arange(head_size, dtype=jnp.int32)[:, None] == head_places[None, :]
    ).astype(full)
    entry = jnp.arange(width, dtype=jnp.int32)
    gain_place = places // weight_rows * gain_rows + entry % weight_rows
    pick = (
        (entry % weight_rows < gain_rows)[:, None]
        & (gain_place[:, None] == jnp.arange(head_size, dtype=jnp.int32)[None, :])
    ).astype(low)
    ordered = dot(window_tokens, order, kind=low)
    own_cotangent = dot(cotangent, order, kind=low)
    other_cotangent = net.pair(own_cotangent)
    chip_cotangent = jnp.concatenate([own_cotangent, other_cotangent])

    z_qkv = net.gather_z(block_qkv)
    down_left = net.plane_second(net.plane_first(block_down[:, :ff_cut], "x"), "y")
    down_right = net.plane_second(net.plane_first(block_down[:, ff_cut:], "y"), "x")
    z_qkv, down_left, down_right, ordered, chip_cotangent, cosines, sines = barrier(
        (z_qkv, down_left, down_right, ordered, chip_cotangent, cosines, sines)
    )
    plane_down = jnp.concatenate(
        [jnp.concatenate(down_left), jnp.concatenate(down_right)], 1
    )

    def cut_planes(blocks, cut):
        return (
            jnp.concatenate([block[:, :cut] for block in blocks]),
            jnp.concatenate([block[:, cut:] for block in blocks]),
        )

    q_left, kv_right = cut_planes(z_qkv, q_cols + 128)
    q_left = net.plane_first(q_left, "y")
    kv_right = net.plane_first(kv_right, "x")
    z_o = net.gather_z(block_o)
    q_left, kv_right, z_o = barrier((q_left, kv_right, z_o))

    q_left = net.plane_second(q_left, "x")
    kv_right = net.plane_second(kv_right, "y")
    o_left, o_right = cut_planes(z_o, o_cut)
    o_left = net.plane_first(o_left, "y")
    o_right = net.plane_first(o_right, "x")
    z_mlp = net.gather_z(block_mlp, 2)
    q_left, kv_right, o_left, o_right, z_mlp = barrier((q_left, kv_right, o_left, o_right, z_mlp))

    o_left = net.plane_second(o_left, "x")
    o_right = net.plane_second(o_right, "y")
    z_mlp = z_mlp + [net.ring(z_mlp[-1], 1)]
    q_parts, kv_parts = net.quarters(q_left), net.quarters(kv_right)
    attn_in, queries, keys, values, query_proj, key_proj, gain_rows_full, heads_gain = project(
        ordered, cosines, sines, pick, q_parts, kv_parts, q_cols, k_cols, halo
    )
    queries, keys, values, o_left, o_right, z_mlp = barrier(
        (queries, keys, values, o_left, o_right, z_mlp)
    )
    gain_one, gain_two = gain_rows_full[0], gain_rows_full[1]

    gate_left, up_right = cut_planes(z_mlp, ff_cols)
    gate_left = net.plane_first(gate_left, "y")
    up_right = net.plane_first(up_right, "x")
    z_down = net.gather_z(plane_down, 1)
    attended = attention_forward(
        queries, keys, values, query_segments, key_segments, row_count, halo, head_size
    )
    attended, gate_left, up_right, z_down = barrier((attended, gate_left, up_right, z_down))

    gate_left = net.plane_second(gate_left, "x")
    up_right = net.plane_second(up_right, "y")
    z_down = z_down[:1] + net.gather_z(z_down[1], 2)
    own_inputs = lax.dynamic_slice_in_dim(ordered, halo + net.core * row_count, row_count).astype(
        full
    )
    o_left, o_right = net.quarters(o_left), net.quarters(o_right)
    which = net.core.astype(jnp.int32).reshape(1)
    branch_sent = net.pair(mix_forward(1 - which, attended, o_left, o_right))
    hidden_state = own_inputs + (mix_forward(which, attended, o_left, o_right) + branch_sent)
    scale_two = inverse_rms(hidden_state)
    normed_two = hidden_state * scale_two
    mlp_own = (normed_two * gain_two).astype(low)
    mlp_other = net.pair(mlp_own)
    mlp_own, mlp_other, gate_left, up_right, z_down = barrier(
        (mlp_own, mlp_other, gate_left, up_right, z_down)
    )

    unit = block_down.shape[0]
    gate_parts, up_parts = net.quarters(gate_left), net.quarters(up_right)
    activated, to_gate, to_up = gate_forward(mlp_own, mlp_other, gate_parts, up_parts)
    mlp_in = jnp.concatenate([mlp_own, mlp_other])
    down_grad = dot(chip_cotangent, activated, 0, 0, low)
    activated, to_gate, to_up, mlp_in, down_grad, z_down = barrier(
        (activated, to_gate, to_up, mlp_in, down_grad, z_down)
    )

    down_a, down_b = net.pieces(down_grad[:, :ff_cut]), net.pieces(down_grad[:, ff_cut:])
    down_a_in = net.scatter_send(down_a, "x")
    down_b_in = net.scatter_send(down_b, "y")
    gate_grad, up_grad, mlp_grad_mine, mlp_grad_other = mlp_backward(
        own_cotangent, other_cotangent, to_gate, to_up, z_down, gate_parts, up_parts, unit
    )
    gate_w_grad = dot(mlp_in, gate_grad, 0, 0, low)
    up_w_grad = dot(mlp_in, up_grad, 0, 0, low)
    mlp_grad_mine, mlp_grad_other, gate_w_grad, up_w_grad, down_a_in, down_b_in = barrier(
        (mlp_grad_mine, mlp_grad_other, gate_w_grad, up_w_grad, down_a_in, down_b_in)
    )

    gate_p, up_p = net.pieces(gate_w_grad), net.pieces(up_w_grad)
    gate_p_in = net.scatter_send(gate_p, "x")
    up_p_in = net.scatter_send(up_p, "y")
    down_a = net.scatter_add(down_a, down_a_in)
    down_b = net.scatter_add(down_b, down_b_in)
    mlp_in_grad = mlp_grad_mine + net.pair(mlp_grad_other)
    hidden_grad = own_cotangent.astype(full) + norm_back(
        mlp_in_grad * gain_two, normed_two, scale_two
    )
    branch_own = hidden_grad.astype(low)
    branch_low = net.by_core(branch_own, net.pair(branch_own))
    attended_grad = mix_backward(branch_low, o_left, o_right)
    o_w_grad = dot(branch_low, attended, 0, 0, low)
    attended_grad, o_w_grad, mlp_in_grad, gate_p_in, up_p_in, down_a, down_b = barrier(
        (attended_grad, o_w_grad, mlp_in_grad, gate_p_in, up_p_in, down_a, down_b)
    )

    gate_p = net.scatter_add(gate_p, gate_p_in)
    up_p = net.scatter_add(up_p, up_p_in)
    down_a_in = net.scatter_send(down_a, "y")
    down_b_in = net.scatter_send(down_b, "x")
    gate_p_in = net.scatter_send(gate_p, "y")
    up_p_in = net.scatter_send(up_p, "x")
    query_low, key_low, value_low, gain_grads = attention_backward(
        queries, keys, values, attended_grad, query_proj, key_proj, cosines, sines, heads_gain,
        query_segments, key_segments, row_count, halo, head_size,
    )
    query_low, key_low, value_low, down_a_in, down_b_in, gate_p_in, up_p_in = barrier(
        (query_low, key_low, value_low, down_a_in, down_b_in, gate_p_in, up_p_in)
    )

    o_a, o_b = net.pieces(o_w_grad[:, :o_cut]), net.pieces(o_w_grad[:, o_cut:])
    o_a_in = net.scatter_send(o_a, "x")
    o_b_in = net.scatter_send(o_b, "y")
    down_a = net.scatter_add(down_a, down_a_in)[(0, 0)]
    down_b = net.scatter_add(down_b, down_b_in)[(0, 0)]
    z_down_in = net.scatter_z(jnp.concatenate([down_a, down_b], 1))
    kv_low = jnp.concatenate([key_low, value_low], axis=1)
    q_w_grad = dot(attn_in[halo:], query_low, 0, 0, low)
    kv_w_grad = dot(attn_in, kv_low, 0, 0, low)
    query_low, kv_low, q_w_grad, kv_w_grad, o_a_in, o_b_in, z_down_in = barrier(
        (query_low, kv_low, q_w_grad, kv_w_grad, o_a_in, o_b_in, z_down_in)
    )

    q_p, kv_p = net.pieces(q_w_grad), net.pieces(kv_w_grad)
    q_p_in = net.scatter_send(q_p, "x")
    kv_p_in = net.scatter_send(kv_p, "y")
    o_a = net.scatter_add(o_a, o_a_in)
    o_b = net.scatter_add(o_b, o_b_in)
    o_a_in = net.scatter_send(o_a, "y")
    o_b_in = net.scatter_send(o_b, "x")
    gate_p = net.scatter_add(gate_p, gate_p_in)[(0, 0)]
    up_p = net.scatter_add(up_p, up_p_in)[(0, 0)]
    z_mlp_in = net.scatter_z(jnp.concatenate([gate_p, up_p], 1))
    q_full = jnp.concatenate([part[:, :q_cols] for part in q_parts])
    kv_full = jnp.concatenate(kv_parts)
    scale_one = inverse_rms(own_inputs)
    normed_one = own_inputs * scale_one
    before_grad = net.chip_along(dot(kv_low[:halo], kv_full, 1, 1, low), -1)
    next_places = net.places(net.chip + 1, 2 * weight_rows)
    next_order = (next_places[:, None] == places[None, :]).astype(low)
    before_grad = dot(before_grad, next_order)
    chip_grad = dot(query_low, q_full, 1, 1) + dot(kv_low[halo:], kv_full, 1, 1)
    chip_grad = jnp.concatenate(
        [chip_grad[: chip_rows - halo], chip_grad[chip_rows - halo :] + before_grad]
    )
    grad_mine, grad_other = net.halves(chip_grad)
    attn_in_grad = grad_mine + net.pair(grad_other)
    gain_one_grad = jnp.sum(attn_in_grad * normed_one, axis=0)
    gain_two_grad = jnp.sum(mlp_in_grad * normed_two, axis=0)
    input_grad = (hidden_grad + norm_back(attn_in_grad * gain_one, normed_one, scale_one)).astype(
        low
    )
    input_grad = dot(input_grad, order, 1, 1, low)
    q_p_in, kv_p_in, o_a_in, o_b_in, z_mlp_in, input_grad, gain_one_grad = barrier(
        (q_p_in, kv_p_in, o_a_in, o_b_in, z_mlp_in, input_grad, gain_one_grad)
    )

    def head_sum(gradient):
        return jnp.sum(head_order * gradient[:, None], axis=0).reshape(net.chips, 2, gain_rows)

    gain_sum = jnp.concatenate(
        [
            gain_one_grad.reshape(net.chips, 2, weight_rows),
            gain_two_grad.reshape(net.chips, 2, weight_rows),
            head_sum(gain_grads[0]),
            head_sum(gain_grads[1]),
        ],
        axis=2,
    )
    gain_p = net.pieces(gain_sum)
    gain_p = net.scatter_add(gain_p, net.scatter_send(gain_p, "x"))
    q_p = net.scatter_add(q_p, q_p_in)
    kv_p = net.scatter_add(kv_p, kv_p_in)
    q_p_in = net.scatter_send(q_p, "y")
    kv_p_in = net.scatter_send(kv_p, "x")
    o_a = net.scatter_add(o_a, o_a_in)[(0, 0)]
    o_b = net.scatter_add(o_b, o_b_in)[(0, 0)]
    z_o_in = net.scatter_z(jnp.concatenate([o_a, o_b], 1))

    def total(blocks):
        return sum([block.astype(full) for block in blocks[1:]], blocks[0].astype(full))

    down_out = net.finish(total(z_down_in))
    mlp_sum = total(z_mlp_in)
    gate_out = net.finish(mlp_sum[:, :ff_cols])
    up_out = net.finish(mlp_sum[:, ff_cols:])
    out_sent = net.pair(down_forward(activated, row_count, z_down, unit, row_count))
    mixed_out = hidden_state + (down_forward(activated, 0, z_down, unit, row_count) + out_sent)
    mixed_out = mixed_out.astype(low)
    mixed_out = dot(mixed_out, order, 1, 1, low)
    q_p_in, kv_p_in, z_o_in, gain_p, down_out, gate_out, up_out, mixed_out = barrier(
        (q_p_in, kv_p_in, z_o_in, gain_p, down_out, gate_out, up_out, mixed_out)
    )

    gain_p = net.scatter_add(gain_p, net.scatter_send(gain_p, "y"))
    gain_sum = total(net.scatter_z(gain_p[(0, 0)])).reshape(2, -1)
    gain_mine, gain_other = net.halves(gain_sum)
    gain_sum = (gain_mine + net.pair(gain_other))[0]
    q_p = net.scatter_add(q_p, q_p_in)[(0, 0)]
    kv_p = net.scatter_add(kv_p, kv_p_in)[(0, 0)]
    qkv_sum = total(net.scatter_z(jnp.concatenate([q_p, kv_p], 1)))
    o_out = net.finish(total(z_o_in))
    return (
        mixed_out,
        input_grad,
        gain_sum[:weight_rows],
        net.finish(qkv_sum[:, :q_cols]),
        net.finish(qkv_sum[:, q_cols : q_cols + k_cols]),
        net.finish(qkv_sum[:, q_cols + k_cols :]),
        o_out,
        gain_sum[2 * weight_rows : 2 * weight_rows + gain_rows],
        gain_sum[2 * weight_rows + gain_rows :],
        gain_sum[weight_rows : 2 * weight_rows],
        gate_out,
        up_out,
        down_out,
    )


def solution(mesh):
    rows = P("dp", None)
    line = P("dp")
    return jax.shard_map(
        per_device,
        mesh=mesh,
        in_specs=(
            rows, line, line, rows, rows, rows, rows, line, line, line, rows, rows, rows, rows,
        ),
        out_specs=(
            rows, rows, line, rows, rows, rows, rows, line, line, line, rows, rows, rows,
        ),
        check_vma=False,
    )
```

```python
import functools
import math

import jax
import jax.numpy as jnp
from jax import lax
from jax.experimental import pallas as pl
from jax.experimental.pallas import tpu as pltpu
from jax.sharding import PartitionSpec as P

epsilon = 1e-06
rope_base = 1000000.0
low = jnp.bfloat16
full = jnp.float32
barrier = lax.optimization_barrier


def dot(left_side, right_side, left_dim=1, right_dim=0, kind=full):
    return lax.dot_general(
        left_side,
        right_side,
        (((left_dim,), (right_dim,)), ((), ())),
        preferred_element_type=kind,
    )


def inverse_rms(values):
    return lax.rsqrt(jnp.mean(values * values, axis=-1, keepdims=True) + epsilon)


def rotate(values, cosines, sines):
    half_size = values.shape[-1] // 2
    first_half = values[..., :half_size]
    second = values[..., half_size:]
    return jnp.concatenate(
        [first_half * cosines - second * sines, second * cosines + first_half * sines], axis=-1
    )


def norm_back(gradient, normed, scales):
    return scales * (gradient - normed * jnp.mean(gradient * normed, axis=-1, keepdims=True))


class Slice:
    def __init__(self):
        self.count = lax.axis_size("dp")
        self.chips = self.count // 2
        self.side = 1
        while 4 * self.side * self.side < self.chips:
            self.side *= 2
        self.device = lax.axis_index("dp")
        self.core = self.device % 2
        self.chip = self.device // 2

    def ring(self, array, by):
        step = 2 * self.side * self.side * by
        return lax.ppermute(
            array, "dp", [(i, (i + step) % self.count) for i in range(self.count)]
        )

    def chip_along(self, array, by):
        pairs = [(i, i + 2 * by) for i in range(self.count) if 0 <= i + 2 * by < self.count]
        return lax.ppermute(array, "dp", pairs)

    def last_core_along(self, array, by):
        pairs = [(i, i + 2 * by) for i in range(1, self.count, 2) if 0 <= i + 2 * by < self.count]
        return lax.ppermute(array, "dp", pairs)

    def pair(self, array):
        return lax.ppermute(array, "dp", [(i, i ^ 1) for i in range(self.count)])

    def plane(self, array, stage, amount):
        pairs = []
        for i in range(self.count):
            along_x = i % 2 != stage % 2
            pairs.append((i, i ^ (2 * amount * (1 if along_x else self.side))))
        return lax.ppermute(array, "dp", pairs)

    def by_core(self, mine, other, axis=0):
        return jnp.where(
            self.core == 0,
            jnp.concatenate([mine, other], axis=axis),
            jnp.concatenate([other, mine], axis=axis),
        )

    def places(self, chip, unit):
        side = self.side
        entry = jnp.arange(self.chips * unit, dtype=jnp.int32)
        inner, block = entry % unit, entry // unit
        along_z, first, second = block % 4, block // 4 % side, block // (4 * side)
        along_x = jnp.where(self.core == 0, second, first)
        along_y = jnp.where(self.core == 0, first, second)
        own_x, own_y, own_z = chip % side, chip // side % side, chip // (side * side)
        source = (
            ((own_z - along_z + 4) % 4) * side * side + (own_y ^ along_y) * side + (own_x ^ along_x)
        )
        return source * unit + inner

    def swapped(self, array):
        size = array.shape[1] // (self.side * self.side)
        starts = [
            (second * self.side + first) * size
            for first in range(self.side)
            for second in range(self.side)
        ]
        return jnp.concatenate([array[:, start : start + size] for start in starts], 1)

    def pair_in(self, array, count):
        return jnp.concatenate([self.pair(part) for part in jnp.split(array, count)])

    def scatter_z(self, blocks):
        return [blocks[0], blocks[1], self.ring(blocks[2], -1), self.ring(blocks[3], 1)]

    def scatter_z_last(self, terms):
        own, one, two, three = terms
        sent = (one.astype(full) + two.astype(full)).astype(one.dtype)
        return [own, three, self.ring(sent, -1)]

    def gather_plane(self, array, stage):
        return [array] + [self.plane(array, stage, m) for m in range(1, self.side)]

    def scatter_plane(self, parts, stage):
        return [self.plane(part, stage, m + 1) for m, part in enumerate(parts[1:])]


def place_kernel(core_ref, mine_ref, other_ref, out_ref):
    at_mine = pl.program_id(0) == core_ref[0]

    @pl.when(at_mine)
    def _():
        out_ref[...] = mine_ref[...]

    @pl.when(jnp.logical_not(at_mine))
    def _():
        out_ref[...] = other_ref[...]


def place(which, mine, other):
    rows, columns = mine.shape
    return call(
        place_kernel,
        "place",
        (2,),
        [whole_block(mine), whole_block(other)],
        [((2 * rows, columns), mine.dtype, mine.shape, lambda i, core: (i, 0))],
        0,
        8 * mine.size,
        scalars=(which,),
    )[0]


def fold_kernel(counts, core_ref, *refs):
    ins, (mine_ref, other_ref) = refs[:-2], refs[-2:]
    rows = mine_ref.shape[0]
    first = core_ref[0] == 0
    start, at = 0, 0
    for count in counts:
        terms = [ref[...].astype(full) for ref in ins[at : at + count]]
        total = sum(terms[1:], terms[0])
        here = slice(start, start + total.shape[1])
        mine_ref[:, here] = jnp.where(first, total[:rows], total[rows:])
        other_ref[:, here] = jnp.where(first, total[rows:], total[:rows])
        start += total.shape[1]
        at += count


def fold(which, *groups):
    rows = groups[0][0].shape[0] // 2
    columns = sum([group[0].shape[1] for group in groups])
    terms = [term for group in groups for term in group]
    fixed = lambda i, core: (0, 0)
    return call(
        functools.partial(fold_kernel, tuple([len(group) for group in groups])),
        "fold",
        (1,),
        [whole_block(term) for term in terms],
        [((rows, columns), full, (rows, columns), fixed)] * 2,
        0,
        20 * rows * columns,
        scalars=(which,),
    )


def join_kernel(ranges, core_ref, mine_ref, other_ref, *outs):
    def write(first, second):
        for out, spans in zip(outs, ranges):
            at = 0
            for ref in (first, second):
                for start, end in spans:
                    out[:, at : at + end - start] = ref[:, start:end]
                    at += end - start

    pl.when(core_ref[0] == 0)(lambda: write(mine_ref, other_ref))
    pl.when(core_ref[0] != 0)(lambda: write(other_ref, mine_ref))


def join(which, mine, other, *ranges):
    rows = mine.shape[0]
    widths = [2 * sum([end - start for start, end in spans]) for spans in ranges]
    fixed = lambda i, core: (0, 0)
    return call(
        functools.partial(join_kernel, ranges),
        "join",
        (1,),
        [whole_block(mine), whole_block(other)],
        [((rows, columns), mine.dtype, (rows, columns), fixed) for columns in widths],
        0,
        16 * mine.size,
        scalars=(which,),
    )


def cut_kernel(cuts, blocks, *refs):
    ins, outs = refs[:blocks], refs[blocks:]
    rows = ins[0].shape[0]
    for at, block in enumerate(ins):
        for out, start, end in zip(outs, cuts[:-1], cuts[1:]):
            out[at * rows : (at + 1) * rows, :] = block[:, start:end]


def stack_cut(blocks, cuts):
    rows, columns = blocks[0].shape
    cuts = (0,) + tuple(cuts) + (columns,)
    shapes = [
        (len(blocks) * rows, end - start) for start, end in zip(cuts[:-1], cuts[1:])
    ]
    return call(
        functools.partial(cut_kernel, cuts, len(blocks)),
        "stack_cut",
        (1,),
        [whole_block(block) for block in blocks],
        [(shape, low, shape, lambda i: (0, 0)) for shape in shapes],
        0,
        4 * len(blocks) * rows * columns,
    )


def score_bias(query_segments, key_segments, rows, halo):
    key_count, query_count = key_segments.shape[0], query_segments.shape[1]
    key_place = lax.broadcasted_iota(jnp.int32, (key_count, query_count), 0) - halo
    query_place = lax.broadcasted_iota(jnp.int32, (key_count, query_count), 1)
    seen = (key_segments == query_segments) & (key_place <= query_place)
    return jnp.where(seen, 0.0, -1e30).astype(full)


def parts_of(rows, halo):
    return (((0, halo), 2 * halo), ((halo, rows), halo + rows))


def reorder(refs, part, parts, unit):
    size = refs[0].shape[0] // parts
    return jnp.concatenate(
        [
            ref[row : row + unit, :]
            for row in range(part * size, (part + 1) * size, unit)
            for ref in refs
        ],
        axis=0,
    )


def write_parts(out_ref, parts, swap=False):
    side = parts.side
    for second in range(side):
        found = parts(second).astype(out_ref.dtype)
        width = found.shape[1]
        if not swap:
            out_ref[:, second * width : (second + 1) * width] = found
            continue
        size = width // side
        for first in range(side):
            start = (first * side + second) * size
            out_ref[:, start : start + size] = found[:, first * size : (first + 1) * size]


class Parts:
    def __init__(self, side, find):
        self.side = side
        self.find = find

    def __call__(self, part):
        return self.find(part)


def contract(value, refs, columns=slice(None)):
    size = refs[0].shape[0]
    total = None
    for at, ref in enumerate(refs):
        term = dot(value[:, at * size : (at + 1) * size], ref[:, columns])
        total = term if total is None else total + term
    return total


def turn(values, cosines, sines):
    return values * cosines + pltpu.roll(values, values.shape[1] // 2, 1) * sines


def row_rms(values):
    return lax.rsqrt(jnp.mean(values * values, axis=1, keepdims=True) + epsilon)


def call(
    kernel, name, grid, ins, outs, flops, bytes_accessed, scratch=(), transcendentals=0, scalars=(),
    least=0,
):
    size = sum([2 * math.prod(block) * array.dtype.itemsize for array, block, _ in ins])
    size += sum([2 * math.prod(block) * jnp.dtype(kind).itemsize for _, kind, block, _ in outs])
    size += sum([math.prod(part.shape) * jnp.dtype(part.dtype).itemsize for part in scratch])
    return pl.pallas_call(
        kernel,
        grid_spec=pltpu.PrefetchScalarGridSpec(
            num_scalar_prefetch=len(scalars),
            grid=grid,
            in_specs=[pl.BlockSpec(block, index) for _, block, index in ins],
            out_specs=[pl.BlockSpec(block, index) for _, _, block, index in outs],
            scratch_shapes=list(scratch),
        ),
        out_shape=[jax.ShapeDtypeStruct(shape, kind) for shape, kind, _, _ in outs],
        compiler_params=pltpu.CompilerParams(vmem_limit_bytes=max(size + (10 << 20), least)),
        cost_estimate=pl.CostEstimate(
            flops=flops, bytes_accessed=bytes_accessed, transcendentals=transcendentals
        ),
        name=name,
    )(*scalars, *[array for array, _, _ in ins])


def tile_of(columns):
    return next(tile for tile in (768, 512, 256, 128, columns) if columns % tile == 0)


def whole_block(array):
    return (array, array.shape, lambda *at: (0,) * array.ndim)


def project_kernel(q_cols, k_cols, x_ref, cos_ref, sin_ref, pick_ref, *refs):
    parts = refs[:-8]
    in_ref, q_ref, k_ref, v_ref, qp_ref, kp_ref, rows_ref, heads_ref = refs[-8:]
    head_size = heads_ref.shape[1]
    k_at = q_cols + 128
    step = pl.program_id(0)

    @pl.when(step == 0)
    def _():
        found = [ref[:, q_cols:k_at].astype(full).T[:8] for ref in parts]
        rows = jnp.concatenate(found, axis=1)
        rows_ref[...] = rows
        heads_ref[...] = dot(rows.astype(low), pick_ref[...])

    x = x_ref[...].astype(full)
    attn_in = (x * row_rms(x) * rows_ref[0:1, :]).astype(low)
    in_ref[...] = attn_in
    cosines, sines = cos_ref[...], sin_ref[...]

    def heads_of(projected, gain, proj_ref, out_ref, start):
        proj_ref[:, start : start + projected.shape[1]] = projected.astype(low)
        for column in range(0, projected.shape[1], head_size):
            head = projected[:, column : column + head_size]
            head = turn(head * row_rms(head) * gain, cosines, sines)
            out_ref[:, start + column : start + column + head_size] = head.astype(low)

    heads_of(contract(attn_in, parts, slice(k_at, k_at + k_cols)), heads_ref[3:4, :], kp_ref, k_ref, 0)
    v_ref[...] = contract(attn_in, parts, slice(k_at + k_cols, k_at + 2 * k_cols)).astype(low)

    @pl.when(step > 0)
    def _():
        for start in range(0, q_cols, 512):
            heads_of(
                contract(attn_in, parts, slice(start, start + 512)),
                heads_ref[2:3, :], qp_ref, q_ref, start,
            )


def project(ordered, cosines, sines, pick, parts, q_cols, k_cols, halo):
    row_count, width = ordered.shape
    own = row_count - halo
    head_size = cosines.shape[1]
    tile = lambda i: (i, 0)
    later = lambda i: (jnp.maximum(i - 1, 0), 0)
    fixed = lambda i: (0, 0)
    return call(
        functools.partial(project_kernel, q_cols, k_cols),
        "project",
        (row_count // halo,),
        [
            (ordered, (halo, width), tile),
            (cosines, (halo, head_size), tile),
            (sines, (halo, head_size), tile),
            whole_block(pick),
        ]
        + [whole_block(part) for part in parts],
        [
            ((row_count, width), low, (halo, width), tile),
            ((own, q_cols), low, (halo, q_cols), later),
            ((row_count, k_cols), low, (halo, k_cols), tile),
            ((row_count, k_cols), low, (halo, k_cols), tile),
            ((own, q_cols), low, (halo, q_cols), later),
            ((row_count, k_cols), low, (halo, k_cols), tile),
            ((8, width), full, (8, width), fixed),
            ((8, head_size), full, (8, head_size), fixed),
        ],
        2 * row_count * width * (q_cols + 2 * k_cols),
        20 << 20,
    )


def gate_kernel(side, xm_ref, xo_ref, *refs):
    gate_refs, up_refs = refs[:side], refs[side : 2 * side]
    act_ref, to_gate_ref, to_up_ref = refs[2 * side :]
    half = xm_ref.shape[0]
    for at, ref in enumerate((xm_ref, xo_ref)):
        rows = slice(at * half, (at + 1) * half)
        gate = contract(ref, gate_refs)
        up = contract(ref, up_refs)
        sigma = 1.0 / (1.0 + jnp.exp(-gate))
        silu = gate * sigma
        act_ref[rows, :] = (silu * up).astype(low)
        to_gate_ref[rows, :] = (up * sigma * (1.0 + gate * (1.0 - sigma))).astype(low)
        to_up_ref[rows, :] = silu.astype(low)


def gate_forward(mine, other, parts):
    half, width = mine.shape
    columns = parts[0].shape[1] // 2
    tile = tile_of(columns)
    wide = lambda j: (0, j)
    after = lambda j: (0, j + columns // tile)
    block = (parts[0].shape[0], tile)
    return call(
        functools.partial(gate_kernel, len(parts)),
        "gate_forward",
        (columns // tile,),
        [whole_block(mine), whole_block(other)]
        + [(part, block, wide) for part in parts]
        + [(part, block, after) for part in parts],
        [((2 * half, columns), low, (2 * half, tile), wide)] * 3,
        8 * half * width * columns,
        16 << 20,
        transcendentals=2 * half * columns,
    )


def act_back_kernel(unit, gb_ref, to_gate_ref, to_up_ref, *refs):
    down_refs, (gate_out, up_out) = refs[:4], refs[4:]
    act_grad = dot(gb_ref[...], reorder(down_refs, 0, 1, unit))
    gate_out[...] = (act_grad * to_gate_ref[...].astype(full)).astype(low)
    up_out[...] = (act_grad * to_up_ref[...].astype(full)).astype(low)


def act_backward(both, to_gate, to_up, down_parts, unit):
    rows, columns = to_gate.shape
    tile = min(tile_of(columns), 512)
    wide = lambda j: (0, j)
    return call(
        functools.partial(act_back_kernel, unit),
        "act_backward",
        (columns // tile,),
        [whole_block(both)]
        + [(factor, (rows, tile), wide) for factor in (to_gate, to_up)]
        + [(part, (part.shape[0], tile), wide) for part in down_parts],
        [((rows, columns), low, (rows, tile), wide)] * 2,
        2 * both.size * columns,
        16 << 20,
    )


def mlp_back_kernel(side, steps, gate_ref, up_ref, *refs):
    parts, (other_ref, mine_ref) = refs[:side], refs[side:]
    columns = gate_ref.shape[1]
    found = Parts(
        side,
        lambda part: dot(gate_ref[...], parts[part][:, :columns], 1, 1)
        + dot(up_ref[...], parts[part][:, columns:], 1, 1),
    )
    pl.when(pl.program_id(0) < steps)(lambda: write_parts(other_ref, found, swap=True))
    pl.when(pl.program_id(0) >= steps)(lambda: write_parts(mine_ref, found))


def mlp_backward(gate_grad, up_grad, parts, tile=256):
    rows, columns = gate_grad.shape[0] // 2, gate_grad.shape[1]
    width = len(parts) * parts[0].shape[0]
    steps = rows // tile
    rows_of = lambda i: ((i + steps) % (2 * steps), 0)
    return call(
        functools.partial(mlp_back_kernel, len(parts), steps),
        "mlp_backward",
        (2 * steps,),
        [(grad, (tile, columns), rows_of) for grad in (gate_grad, up_grad)]
        + [whole_block(part) for part in parts],
        [
            ((rows, width), full, (tile, width), lambda i: (jnp.minimum(i, steps - 1), 0)),
            ((rows, width), full, (tile, width), lambda i: (jnp.maximum(i - steps, 0), 0)),
        ],
        8 * rows * columns * width,
        16 << 20,
    )


def down_kernel(side, unit, steps, act_ref, *refs):
    down_refs, (other_ref, mine_ref) = refs[:4], refs[4:]
    parts = Parts(
        side, lambda part: dot(act_ref[...], reorder(down_refs, part, side, unit), 1, 1)
    )
    pl.when(pl.program_id(0) < steps)(lambda: write_parts(other_ref, parts, swap=True))
    pl.when(pl.program_id(0) >= steps)(lambda: write_parts(mine_ref, parts))


def down_forward(activated, down_parts, side, unit, tile=256):
    rows, columns = activated.shape[0] // 2, activated.shape[1]
    width = 4 * down_parts[0].shape[0]
    steps = rows // tile
    return call(
        functools.partial(down_kernel, side, unit, steps),
        "down_forward",
        (2 * steps,),
        [(activated, (tile, columns), lambda i: ((i + steps) % (2 * steps), 0))]
        + [whole_block(part) for part in down_parts],
        [
            ((rows, width), full, (tile, width), lambda i: (jnp.minimum(i, steps - 1), 0)),
            ((rows, width), full, (tile, width), lambda i: (jnp.maximum(i - steps, 0), 0)),
        ],
        4 * rows * columns * width,
        12 << 20,
    )


def back_kernel(side, q_cols, steps, core_ref, q_ref, k_ref, v_ref, halo_ref, *refs):
    parts, (other_ref, mine_ref) = refs[:side], refs[side:]
    step = pl.program_id(0)
    k_cols = k_ref.shape[1]
    k_at = q_cols + 128
    v_at = k_at + k_cols
    half = jnp.where(step < steps, 1 - core_ref[0], core_ref[0])
    last = (half == 1) & (step % steps == steps - 1)
    later = jnp.where(last, halo_ref[...].astype(full), 0.0)
    keys = (k_ref[...].astype(full) + later[:, :k_cols]).astype(low)
    values = (v_ref[...].astype(full) + later[:, k_cols:]).astype(low)

    def terms(part):
        return (
            dot(q_ref[...], parts[part][:, :q_cols], 1, 1)
            + dot(keys, parts[part][:, k_at:v_at], 1, 1)
            + dot(values, parts[part][:, v_at : v_at + k_cols], 1, 1)
        )

    pl.when(step < steps)(lambda: write_parts(other_ref, Parts(side, terms), swap=True))
    pl.when(step >= steps)(lambda: write_parts(mine_ref, Parts(side, terms)))


def input_backward(which, query_low, key_low, value_low, later, parts):
    own, q_cols = query_low.shape
    k_cols = key_low.shape[1]
    tile = later.shape[0]
    halo_steps = (key_low.shape[0] - own) // tile
    steps = own // 2 // tile
    width = len(parts) * parts[0].shape[0]

    def own_rows(i, core):
        half = jnp.where(i < steps, 1 - core[0], core[0])
        return half * steps + i % steps

    return call(
        functools.partial(back_kernel, len(parts), q_cols, steps),
        "input_backward",
        (2 * steps,),
        [(query_low, (tile, q_cols), lambda i, core: (own_rows(i, core), 0))]
        + [
            (part, (tile, k_cols), lambda i, core: (halo_steps + own_rows(i, core), 0))
            for part in (key_low, value_low)
        ]
        + [whole_block(part) for part in [later] + parts],
        [
            ((own // 2, width), full, (tile, width), lambda i, core: (jnp.minimum(i, steps - 1), 0)),
            ((own // 2, width), full, (tile, width), lambda i, core: (jnp.maximum(i - steps, 0), 0)),
        ],
        2 * own * width * (q_cols + 2 * k_cols),
        16 << 20,
        scalars=(which,),
    )


def finish_kernel(mine_ref, sent_ref, x_ref, hidden_ref, gain_ref, out_ref, sum_ref):
    grad = mine_ref[...] + sent_ref[...]
    x = x_ref[...].astype(full)
    scales = row_rms(x)
    normed = x * scales

    @pl.when(pl.program_id(0) == 0)
    def _():
        sum_ref[...] = jnp.zeros_like(sum_ref)

    sum_ref[0:1, :] += jnp.sum(grad * normed, axis=0, keepdims=True)
    back = grad * gain_ref[0:1, :]
    mean = jnp.mean(back * normed, axis=1, keepdims=True)
    out_ref[...] = (hidden_ref[...] + scales * (back - normed * mean)).astype(low)


def finish_tokens(mine, sent, inputs, hidden_grad, gains, tile=128):
    rows, width = mine.shape
    rows_of = lambda i: (i, 0)
    fixed = lambda i: (0, 0)
    return call(
        finish_kernel,
        "finish_tokens",
        (rows // tile,),
        [(array, (tile, width), rows_of) for array in (mine, sent, inputs, hidden_grad)]
        + [whole_block(gains)],
        [((rows, width), low, (tile, width), rows_of), ((8, width), full, (8, width), fixed)],
        12 * rows * width,
        18 * rows * width,
    )


def sums_kernel(side, tokens, segments, *refs):
    outs, turned = refs[-1 - side : -1], refs[-1]
    right_refs = refs[-1 - side - len(segments) : -1 - side]
    left_refs = refs[: -1 - side - len(segments)]
    step = pl.program_id(0)
    size = turned.shape[0] // side

    @pl.when(step == 0)
    def _():
        start = 0
        for ref in left_refs:
            turned[:, start : start + ref.shape[0]] = ref[...].T
            start += ref.shape[0]

    for ref, (first, steps, row) in zip(right_refs, segments):

        @pl.when((step >= first) & (step < first + steps))
        def _(ref=ref, row=row):
            for part, out in enumerate(outs):
                out[...] = dot(turned[part * size : (part + 1) * size, row:], ref[...]).astype(low)


def token_sums(side, lefts, rights):
    width = lefts[0].shape[1]
    tokens = sum([left.shape[0] for left in lefts])
    tile = min([tile_of(array.shape[1]) for array, _ in rights])
    segments, step = [], 0
    for array, row in rights:
        steps = array.shape[1] // tile
        segments.append((step, steps, row))
        step += steps

    def clip(first, steps):
        return lambda j: (0, jnp.clip(j - first, 0, steps - 1))

    ins = [whole_block(left) for left in lefts]
    for (array, _), (first, steps, _) in zip(rights, segments):
        ins.append((array, (array.shape[0], tile), clip(first, steps)))
    found = call(
        functools.partial(sums_kernel, side, tokens, tuple(segments)),
        "token_sums",
        (step,),
        ins,
        [((width // side, step * tile), low, (width // side, tile), lambda j: (0, j))] * side,
        2 * tokens * width * step * tile,
        12 << 20,
        scratch=[pltpu.VMEM((width, tokens), low)],
    )
    return list(found)


def mix_kernel(side, steps, core_ref, att_left, att_right, *refs):
    weights, (other_ref, mine_ref) = refs[:side], refs[side:]
    cut = att_left.shape[1]
    parts = Parts(
        side,
        lambda part: dot(att_left[...], weights[part][:, :cut], 1, 1)
        + dot(att_right[...], weights[part][:, cut:], 1, 1),
    )
    pl.when(pl.program_id(0) < steps)(lambda: write_parts(other_ref, parts, swap=True))
    pl.when(pl.program_id(0) >= steps)(lambda: write_parts(mine_ref, parts))


def mix_forward(which, att_left, att_right, weights, tile=256):
    rows, columns = att_left.shape[0] // 2, att_left.shape[1]
    width = len(weights) * weights[0].shape[0]
    steps = rows // tile

    def rows_of(i, core):
        half = jnp.where(i < steps, 1 - core[0], core[0])
        return (half * steps + i % steps, 0)

    return call(
        functools.partial(mix_kernel, len(weights), steps),
        "mix_forward",
        (2 * steps,),
        [(part, (tile, columns), rows_of) for part in (att_left, att_right)]
        + [whole_block(part) for part in weights],
        [
            ((rows, width), full, (tile, width), lambda i, core: (jnp.minimum(i, steps - 1), 0)),
            ((rows, width), full, (tile, width), lambda i, core: (jnp.maximum(i - steps, 0), 0)),
        ],
        8 * rows * columns * width,
        12 << 20,
        scalars=(which,),
    )


def mix_back_kernel(branch_ref, *refs):
    weights, out_ref = refs[:-1], refs[-1]
    out_ref[...] = contract(branch_ref, weights).astype(low)


def mix_backward(branch, weights, tile=256):
    rows, width = branch.shape
    columns = weights[0].shape[1]
    rows_of = lambda i: (i, 0)
    return call(
        mix_back_kernel,
        "mix_backward",
        (rows // tile,),
        [(branch, (tile, width), rows_of)] + [whole_block(part) for part in weights],
        [((rows, columns), low, (tile, columns), rows_of)],
        2 * rows * columns * width,
        6 << 20,
    )[0]


def forward_kernel(scale, rows, halo, q_ref, k_ref, v_ref, qs_ref, ks_ref, out_ref, bias_ref):
    block = pl.program_id(1)
    start = pl.multiple_of(block * rows, rows)
    window = halo + rows
    head_size = k_ref.shape[1]

    @pl.when(pl.program_id(0) == 0)
    def _():
        bias_ref[block] = score_bias(
            qs_ref[...], ks_ref[pl.ds(start, window), :], rows, halo
        )

    for (low_row, high_row), key_count in parts_of(rows, halo):
        keys = k_ref[pl.ds(start, key_count), :]
        values = v_ref[pl.ds(start, key_count), :]
        bias = bias_ref[block, :key_count, low_row:high_row]
        for group in range(q_ref.shape[1] // head_size):
            lanes = slice(group * head_size, (group + 1) * head_size)
            query = q_ref[low_row:high_row, lanes]
            scores = dot(keys, query, 1, 1) * scale + bias
            weights = jnp.exp2(scores)
            total = jnp.sum(weights, axis=0, keepdims=True)
            probs = (weights * (1.0 / total)).astype(low)
            mixed = dot(values, probs, 0, 0)
            out_ref[low_row:high_row, lanes] = mixed.T.astype(low)


def head_back(gradient, projected, gain, cosines, sines):
    scales = row_rms(projected)
    normed = projected * scales
    back = turn(gradient, cosines, -sines)
    gain_grad = jnp.sum(back * normed, axis=0, keepdims=True)
    back = back * gain
    mean = jnp.mean(back * normed, axis=1, keepdims=True)
    return scales * (back - normed * mean), gain_grad


def backward_kernel(
    scale, rows, halo, *refs
):
    q_ref, k_ref, v_ref, g_ref, qp_ref, kp_ref, cos_ref, sin_ref, heads_ref, qs_ref, ks_ref = refs[
        :11
    ]
    dq_ref, dk_ref, dv_ref, gains_ref, bias_ref, key_ref, value_ref = refs[11:]
    head = pl.program_id(0)
    block = pl.program_id(1)
    start = pl.multiple_of(block * rows, rows)
    window = halo + rows
    head_size = k_ref.shape[1]
    factor = head_size ** (-0.5)

    @pl.when(head == 0)
    def _():
        bias_ref[block] = score_bias(
            qs_ref[...], ks_ref[pl.ds(start, window), :], rows, halo
        )

    @pl.when((head == 0) & (block == 0))
    def _():
        gains_ref[...] = jnp.zeros_like(gains_ref)

    @pl.when(block == 0)
    def _():
        key_ref[...] = jnp.zeros_like(key_ref)
        value_ref[...] = jnp.zeros_like(value_ref)

    for (low_row, high_row), key_count in parts_of(rows, halo):
        keys = k_ref[pl.ds(start, key_count), :]
        values = v_ref[pl.ds(start, key_count), :]
        bias = bias_ref[block, :key_count, low_row:high_row]
        here = pl.ds(start + (halo + low_row), high_row - low_row)
        cosines, sines = cos_ref[here, :], sin_ref[here, :]
        key_sum = None
        value_sum = None
        for group in range(q_ref.shape[1] // head_size):
            lanes = slice(group * head_size, (group + 1) * head_size)
            query = q_ref[low_row:high_row, lanes]
            grad = g_ref[low_row:high_row, lanes]
            weights = jnp.exp2(dot(keys, query, 1, 1) * scale + bias)
            total = jnp.sum(weights, axis=0, keepdims=True)
            softmax = weights * (1.0 / total)
            prob_grad = dot(values, grad, 1, 1)
            product = softmax * prob_grad
            mean = jnp.sum(product, axis=0, keepdims=True)
            score_grad = (product - softmax * mean).astype(low)
            value_term = dot(softmax.astype(low), grad)
            key_term = dot(score_grad, query)
            value_sum = value_term if value_sum is None else value_sum + value_term
            key_sum = key_term if key_sum is None else key_sum + key_term
            query_grad = dot(keys, score_grad, 0, 0).T * factor
            query_grad, gain_grad = head_back(
                query_grad,
                qp_ref[low_row:high_row, lanes].astype(full),
                heads_ref[2:3, :],
                cosines,
                sines,
            )
            dq_ref[low_row:high_row, lanes] = query_grad.astype(low)
            gains_ref[0:1, :] += gain_grad
        key_ref[pl.ds(start, key_count), :] += key_sum * factor
        value_ref[pl.ds(start, key_count), :] += value_sum

    @pl.when(block == pl.num_programs(1) - 1)
    def _():
        dv_ref[...] = value_ref[...].astype(low)
        for row in range(0, k_ref.shape[0], halo):
            here = slice(row, row + halo)
            key_grad, gain_grad = head_back(
                key_ref[here, :],
                kp_ref[here, :].astype(full),
                heads_ref[3:4, :],
                cos_ref[here, :],
                sin_ref[here, :],
            )
            dk_ref[here, :] = key_grad.astype(low)
            gains_ref[1:2, :] += gain_grad


def attention_forward(
    queries, keys, values, query_segments, key_segments, rows, halo, head_size, first, heads
):
    token_count = queries.shape[0]
    lanes = queries.shape[1] // (keys.shape[1] // head_size)
    window = halo + token_count
    scale = head_size ** (-0.5) / math.log(2.0)
    q_at, k_at = lambda h, b: (b, first + h), lambda h, b: (0, first + h)
    shape = (token_count, heads * lanes)
    return call(
        functools.partial(forward_kernel, scale, rows, halo),
        "attention_forward",
        (heads, token_count // rows),
        [
            (queries, (rows, lanes), q_at),
            (keys, (window, head_size), k_at),
            (values, (window, head_size), k_at),
            (query_segments, (1, rows), lambda h, b: (0, b)),
            whole_block(key_segments),
        ],
        [(shape, low, (rows, lanes), lambda h, b: (b, h))],
        4 * token_count * heads * lanes * (halo + rows),
        4 << 20,
        scratch=[pltpu.VMEM((token_count // rows, halo + rows, rows), full)],
        transcendentals=token_count * heads * lanes // head_size * (halo + rows),
    )[0]


def attention_backward(
    queries, keys, values, grads, query_proj, key_proj, cosines, sines, heads_gain,
    query_segments, key_segments, rows, halo, head_size,
):
    token_count = queries.shape[0]
    heads = keys.shape[1] // head_size
    lanes = queries.shape[1] // heads
    window = halo + token_count
    scale = head_size ** (-0.5) / math.log(2.0)
    q_at, k_at, fixed = lambda h, b: (b, h), lambda h, b: (0, h), lambda h, b: (0, 0)
    return call(
        functools.partial(backward_kernel, scale, rows, halo),
        "attention_backward",
        (heads, token_count // rows),
        [
            (queries, (rows, lanes), q_at),
            (keys, (window, head_size), k_at),
            (values, (window, head_size), k_at),
            (grads, (rows, lanes), q_at),
            (query_proj, (rows, lanes), q_at),
            (key_proj, (window, head_size), k_at),
            whole_block(cosines),
            whole_block(sines),
            whole_block(heads_gain),
            (query_segments, (1, rows), lambda h, b: (0, b)),
            whole_block(key_segments),
        ],
        [
            (queries.shape, low, (rows, lanes), q_at),
            (keys.shape, low, (window, head_size), k_at),
            (keys.shape, low, (window, head_size), k_at),
            ((8, head_size), full, (8, head_size), fixed),
        ],
        10 * queries.size * (halo + rows),
        24 << 20,
        scratch=[
            pltpu.VMEM((token_count // rows, halo + rows, rows), full),
            pltpu.VMEM((window, head_size), full),
            pltpu.VMEM((window, head_size), full),
        ],
        least=48 << 20,
        transcendentals=queries.size // head_size * (halo + rows),
    )


def per_device(
    tokens,
    segments,
    norm_gain,
    q_weight,
    k_weight,
    v_weight,
    o_weight,
    q_gain,
    k_gain,
    mlp_gain,
    gate_weight,
    up_weight,
    down_weight,
    cotangent,
):
    net = Slice()
    row_count, width = tokens.shape
    halo = row_count // 2
    chip_rows = 2 * row_count
    weight_rows = q_weight.shape[0]
    head_size = q_gain.shape[0] * net.count
    gain_rows = q_gain.shape[0]

    q_cols, k_cols, o_cols, ff_cols = (
        weight.shape[1] // 2 for weight in (q_weight, k_weight, o_weight, gate_weight)
    )
    unit = 2 * weight_rows
    side = net.side
    which = net.core.astype(jnp.int32).reshape(1)

    column = lax.broadcasted_iota(jnp.int32, (weight_rows, 128), 1)
    extras = jnp.zeros((weight_rows, 128), low)
    for at, gain in enumerate((norm_gain, mlp_gain, q_gain, k_gain)):
        gain = jnp.pad(gain, (0, weight_rows - gain.shape[0]))
        extras = jnp.where(column == at, gain[:, None], extras)

    def chip_block(*parts):
        mine, other = [], []
        for weight, start, end in parts:
            half = weight.shape[1] // 2 if end is not None else 0
            for to, core in ((mine, net.core), (other, 1 - net.core)):
                if end is None:
                    to.append(weight)
                else:
                    to.append(
                        lax.dynamic_slice_in_dim(weight, core * half + start, end - start, 1)
                    )
        return net.by_core(jnp.concatenate(mine, 1), net.pair(jnp.concatenate(other, 1)))

    block_qkv = chip_block(
        (q_weight, 0, q_cols), (extras, 0, None), (k_weight, 0, k_cols), (v_weight, 0, k_cols)
    )
    z_qkv = [block_qkv, net.ring(block_qkv, 1), net.ring(block_qkv, -1)]
    z_one, z_three, tokens, segments, o_weight, gate_weight, up_weight, down_weight = barrier(
        (
            z_qkv[1], z_qkv[2], tokens, segments, o_weight, gate_weight, up_weight, down_weight
        )
    )
    z_qkv = [block_qkv, z_one, net.ring(z_one, 1), z_three]
    block_rest = chip_block(
        (down_weight, 0, ff_cols), (o_weight, 0, o_cols), (gate_weight, 0, ff_cols),
        (up_weight, 0, ff_cols),
    )
    block_down, block_mlp = block_rest[:, :ff_cols], block_rest[:, ff_cols:]
    z_mlp = [block_mlp, net.ring(block_mlp, 1)]
    numbers = jnp.broadcast_to(segments.astype(low)[:, None], (row_count, 128))
    own_tokens = jnp.concatenate([tokens, numbers], 1)
    before = net.last_core_along(own_tokens[row_count - halo :], 1)
    places = net.places(net.chip, unit)
    order = (jnp.arange(width, dtype=jnp.int32)[:, None] == places[None, :]).astype(low)
    head_places = net.places(net.chip, 2 * gain_rows)
    head_order = (
        jnp.arange(head_size, dtype=jnp.int32)[:, None] == head_places[None, :]
    ).astype(full)
    entry = jnp.arange(width, dtype=jnp.int32)
    gain_place = places // weight_rows * gain_rows + entry % weight_rows
    pick = (
        (entry % weight_rows < gain_rows)[:, None]
        & (gain_place[:, None] == jnp.arange(head_size, dtype=jnp.int32)[None, :])
    ).astype(low)
    plane_down = jnp.stack(net.gather_plane(block_down, 0))
    z_qkv, plane_down, own_tokens, before, order, pick, z_mlp, cotangent = barrier(
        (z_qkv, plane_down, own_tokens, before, order, pick, z_mlp, cotangent)
    )

    (qkv,) = stack_cut(z_qkv, ())
    qkv = net.gather_plane(qkv, 0)
    z_mlp.append(net.ring(z_mlp[-1], 1))
    plane_down = jnp.stack(net.gather_plane(plane_down, 1))
    plane_down = plane_down.reshape(side * side * unit, ff_cols)
    both = place(which, own_tokens, net.pair(own_tokens))
    before = jnp.where(net.core == 0, net.pair(before), before)
    qkv, z_mlp, plane_down, both, before = barrier((qkv, z_mlp, plane_down, both, before))

    (qkv,) = stack_cut(qkv, ())
    qkv = net.gather_plane(qkv, 1)
    z_mlp.append(net.ring(z_mlp[-1], 1))
    chip_tokens, before_tokens = both[:, :width], before[:, :width]
    chip_segments = both[:, width].astype(jnp.int32)
    before_segments = jnp.where(net.chip > 0, before[:, width].astype(jnp.int32), -1)
    window_tokens = jnp.concatenate([before_tokens, chip_tokens])
    window_segments = jnp.concatenate([before_segments, chip_segments])
    counter = jnp.arange(halo + chip_rows, dtype=jnp.int32)
    changes = jnp.concatenate([jnp.ones((1,), bool), window_segments[1:] != window_segments[:-1]])
    starts = lax.cummax(jnp.where(changes, counter, 0), axis=0)
    offsets = (counter - starts).astype(full)
    frequency = jnp.exp(
        (jnp.arange(head_size, dtype=jnp.int32) % (head_size // 2)).astype(full)
        * (-2.0 * math.log(rope_base) / head_size)
    )
    angles = offsets[:, None] * frequency[None, :]
    cosines = jnp.cos(angles)
    sines = jnp.sin(angles) * jnp.where(jnp.arange(head_size) < head_size // 2, -1.0, 1.0)
    query_segments = chip_segments[None, :]
    key_segments = window_segments[:, None]
    ordered = dot(window_tokens, order, kind=low)
    qkv, z_mlp, plane_down, ordered, cosines, sines = barrier(
        (qkv, z_mlp, plane_down, ordered, cosines, sines)
    )

    own_cotangent = dot(cotangent, order, kind=low)
    (mlp,) = stack_cut(z_mlp, ())
    mlp = net.gather_plane(mlp, 0)
    z_down = [plane_down, net.ring(plane_down, 1)]
    attn_in, queries, keys, values, query_proj, key_proj, gain_rows_full, heads_gain = project(
        ordered, cosines, sines, pick, qkv, q_cols, k_cols, halo
    )
    gain_one, gain_two = gain_rows_full[0], gain_rows_full[1]
    kv_heads = k_cols // head_size

    def attend(first):
        return attention_forward(
            queries, keys, values, query_segments, key_segments, row_count, halo, head_size,
            first, kv_heads // 2,
        )

    att_left = attend(0)
    att_left, mlp, z_down, queries, keys, values, own_cotangent = barrier(
        (att_left, mlp, z_down, queries, keys, values, own_cotangent)
    )

    other_cotangent = net.pair(net.swapped(own_cotangent))
    cotangents = jnp.concatenate([own_cotangent, other_cotangent])
    mix, mlp = stack_cut(mlp, (o_cols,))
    mix = net.gather_plane(mix, 1)
    att_right = attend(kv_heads // 2)
    z_down.append(net.ring(z_down[-1], 1))
    att_left, att_right, mix, mlp, cotangents, z_down = barrier(
        (att_left, att_right, mix, mlp, cotangents, z_down)
    )

    mlp = net.gather_plane(mlp, 1)
    z_down.append(net.ring(z_down[-1], 1))
    own_inputs = lax.dynamic_slice_in_dim(ordered, halo + net.core * row_count, row_count).astype(
        full
    )
    branch_other, branch_mine = mix_forward(which, att_left, att_right, mix)
    hidden_state = own_inputs + (branch_mine + net.pair_in(branch_other, 4))
    scale_two = inverse_rms(hidden_state)
    normed_two = hidden_state * scale_two
    mlp_own = (normed_two * gain_two).astype(low)
    mlp_other = net.pair_in(net.swapped(mlp_own), 2)
    mlp_own, mlp_other, mlp, z_down = barrier((mlp_own, mlp_other, mlp, z_down))

    activated, to_gate, to_up = gate_forward(mlp_own, mlp_other, mlp)
    down_sums = token_sums(side, [cotangents], [(activated, 0)])
    activated, to_gate, to_up, down_sums, z_down = barrier(
        (activated, to_gate, to_up, down_sums, z_down)
    )

    def plus(array, *terms):
        return sum([term.astype(full) for term in terms], array.astype(full)).astype(array.dtype)

    def inner(terms):
        size = terms[0].shape[0] // side
        sent = [
            plus(*[term[at * size : (at + 1) * size] for term in terms]) for at in range(1, side)
        ]
        return [term[:size] for term in terms], [None] + sent

    down_in = net.scatter_plane(down_sums, 1)
    gate_grad, up_grad = act_backward(cotangents, to_gate, to_up, z_down, unit)
    mlp_sums = token_sums(side, [mlp_own, mlp_other], [(gate_grad, 0), (up_grad, 0)])
    gate_grad, up_grad, mlp_sums, down_sum, activated = barrier(
        (gate_grad, up_grad, mlp_sums, down_sums[:1] + down_in, activated)
    )

    mlp_in = net.scatter_plane(mlp_sums, 1)
    z_down_sum = plus(*down_sum).reshape(side, 4, unit, ff_cols)
    z_down_sum = net.scatter_z([z_down_sum[:, m] for m in range(4)])
    mlp_grad_other, mlp_grad_mine = mlp_backward(gate_grad, up_grad, mlp)
    mlp_in_grad = mlp_grad_mine + net.pair_in(mlp_grad_other, 4)
    hidden_grad = own_cotangent.astype(full) + norm_back(
        mlp_in_grad * gain_two, normed_two, scale_two
    )
    branch_own = hidden_grad.astype(low)
    branch_low = place(which, branch_own, net.pair_in(net.swapped(branch_own), 2))
    attended_grad = mix_backward(branch_low, mix)
    mix_sums = token_sums(side, [branch_low], [(att_left, 0), (att_right, 0)])
    out_other, out_mine = down_forward(activated, z_down, side, unit)
    mixed_out = hidden_state + (out_mine + net.pair_in(out_other, 4))
    mixed_out = dot(mixed_out.astype(low), order, 1, 1, low)
    attended_grad, mix_sums, mlp_in_grad, mlp_sum, mixed_out, z_down_sum = barrier(
        (attended_grad, mix_sums, mlp_in_grad, mlp_sums[:1] + mlp_in, mixed_out, z_down_sum)
    )

    mlp_sum, mlp_sent = inner(mlp_sum)
    mlp_in = net.scatter_plane(mlp_sent, 0)
    mix_in = net.scatter_plane(mix_sums, 1)
    z_down_sum = net.scatter_z_last(z_down_sum)
    query_low, key_low, value_low, gain_grads = attention_backward(
        queries, keys, values, attended_grad, query_proj, key_proj, cosines, sines, heads_gain,
        query_segments, key_segments, row_count, halo, head_size,
    )
    query_low, key_low, value_low, mlp_sum, mix_sum, z_down_sum = barrier(
        (query_low, key_low, value_low, mlp_sum + mlp_in, mix_sums[:1] + mix_in, z_down_sum)
    )

    mix_sum, mix_sent = inner(mix_sum)
    mix_in = net.scatter_plane(mix_sent, 0)
    z_mlp = jnp.split(plus(*mlp_sum), 4)
    down_sum = plus(*z_down_sum)
    down_in = net.scatter_plane([down_sum[m] for m in range(side)], 0)
    later = net.chip_along(jnp.concatenate([key_low[:halo], value_low[:halo]], 1), -1)
    qkv_sums = token_sums(side, [attn_in], [(query_low, halo), (key_low, 0), (value_low, 0)])
    qkv_sums, query_low, mlp_in_grad, mix_sum, z_mlp, down_sum, later = barrier(
        (
            qkv_sums, query_low, mlp_in_grad, mix_sum + mix_in, z_mlp, [down_sum[0]] + down_in,
            later,
        )
    )

    qkv_in = net.scatter_plane(qkv_sums, 1)
    z_mlp = net.scatter_z(z_mlp)
    gain_two_grad = jnp.sum(mlp_in_grad * normed_two, axis=0, keepdims=True)
    head_gains = dot(gain_grads[:2], head_order)
    z_mix = jnp.split(plus(*mix_sum), 4)
    grad_other, grad_mine = input_backward(which, query_low, key_low, value_low, later, qkv)
    qkv_sum, z_mlp, grad_other, grad_mine, z_mix, gain_two_grad, head_gains = barrier(
        (
            qkv_sums[:1] + qkv_in, z_mlp, grad_other, grad_mine, z_mix, gain_two_grad, head_gains,
        )
    )

    qkv_sum, qkv_sent = inner(qkv_sum)
    qkv_in = net.scatter_plane(qkv_sent, 0)
    z_mlp = net.scatter_z_last(z_mlp)
    z_mix = net.scatter_z(z_mix)
    grad_sent = net.pair(grad_other)
    qkv_sum, z_mlp, z_mix, grad_mine, grad_sent = barrier(
        (qkv_sum + qkv_in, z_mlp, z_mix, grad_mine, grad_sent)
    )

    z_qkv = jnp.split(plus(*qkv_sum), 4)
    z_qkv = [z_qkv[0]] + [net.ring(z_qkv[m], -m) for m in range(1, 4)]
    z_mix = net.scatter_z_last(z_mix)
    input_grad, gain_one_grad = finish_tokens(
        grad_mine, grad_sent, own_inputs, hidden_grad, gain_rows_full
    )
    gains = jnp.concatenate([gain_one_grad[:1], gain_two_grad])

    def gain_parts(gains, heads):
        count = side if gains.shape[1] > width // (side * side) else 4
        return [
            jnp.concatenate(both, 1)
            for both in zip(jnp.split(gains, count, 1), jnp.split(heads, count, 1))
        ]

    def gain_cut(array):
        at = array.shape[1] * width // (width + head_size)
        return array[:, :at], array[:, at:]

    gains = gain_parts(gains, head_gains)
    gains = plus(gains[0], *net.scatter_plane(gains, 1))
    gains = gain_parts(*gain_cut(gains))
    gains = plus(gains[0], *net.scatter_plane(gains, 0))
    rest_mine, rest_other = fold(which, z_mlp, down_sum)
    rest_other = net.pair(rest_other)
    z_qkv, gains, rest_mine, rest_other, input_grad, z_mix = barrier(
        (z_qkv, gains, rest_mine, rest_other, input_grad, z_mix)
    )

    input_grad = dot(input_grad, order, 1, 1, low)
    z_mine, z_other = fold(which, z_qkv, z_mix)
    z_other = net.pair(z_other)
    gains = gain_parts(*gain_cut(gains))
    gains = sum([net.ring(gains[m], -m) for m in range(1, 4)], gains[0])
    gains, heads = gain_cut(gains)
    gains = jnp.concatenate(
        [gains[:1, :weight_rows], gains[1:, :weight_rows], heads[:1, :gain_rows],
         heads[1:, :gain_rows], gains[:1, weight_rows:], gains[1:, weight_rows:],
         heads[:1, gain_rows:], heads[1:, gain_rows:]], 1,
    ).reshape(2, -1)
    gain_mine = jnp.where(net.core == 0, gains[0], gains[1])
    gain_other = jnp.where(net.core == 0, gains[1], gains[0])
    gain_sum = gain_mine + net.pair(gain_other)
    ends = [0]
    for size in (ff_cols, ff_cols, ff_cols):
        ends.append(ends[-1] + size)
    gate_out, up_out, down_out = join(
        which, rest_mine, rest_other, *[((start, end),) for start, end in zip(ends[:-1], ends[1:])]
    )
    v_at = q_cols + k_cols
    o_at = v_at + k_cols
    q_out, k_out, v_out, o_out = join(
        which, z_mine, z_other, ((0, q_cols),), ((q_cols, v_at),), ((v_at, o_at),),
        ((o_at, o_at + o_cols),),
    )
    return (
        mixed_out,
        input_grad,
        gain_sum[:weight_rows],
        q_out,
        k_out,
        v_out,
        o_out,
        gain_sum[2 * weight_rows : 2 * weight_rows + gain_rows],
        gain_sum[2 * weight_rows + gain_rows :],
        gain_sum[weight_rows : 2 * weight_rows],
        gate_out,
        up_out,
        down_out,
    )


def solution(mesh):
    rows = P("dp", None)
    line = P("dp")
    return jax.shard_map(
        per_device,
        mesh=mesh,
        in_specs=(
            rows, line, line, rows, rows, rows, rows, line, line, line, rows, rows, rows, rows,
        ),
        out_specs=(
            rows, rows, line, rows, rows, rows, rows, line, line, line, rows, rows, rows,
        ),
        check_vma=False,
    )
```

```python
import functools
import math

import jax
import jax.numpy as jnp
from jax import lax
from jax.experimental import pallas as pl
from jax.experimental.pallas import tpu as pltpu
from jax.sharding import PartitionSpec as P

epsilon = 1e-06
rope_base = 1000000.0
low = jnp.bfloat16
full = jnp.float32
barrier = lax.optimization_barrier


def dot(left_side, right_side, left_dim=1, right_dim=0, kind=full):
    return lax.dot_general(
        left_side,
        right_side,
        (((left_dim,), (right_dim,)), ((), ())),
        preferred_element_type=kind,
    )


def inverse_rms(values):
    return lax.rsqrt(jnp.mean(values * values, axis=-1, keepdims=True) + epsilon)


def rotate(values, cosines, sines):
    half_size = values.shape[-1] // 2
    first_half = values[..., :half_size]
    second = values[..., half_size:]
    return jnp.concatenate(
        [first_half * cosines - second * sines, second * cosines + first_half * sines], axis=-1
    )


def norm_back(gradient, normed, scales):
    return scales * (gradient - normed * jnp.mean(gradient * normed, axis=-1, keepdims=True))


class Slice:
    def __init__(self):
        self.count = lax.axis_size("dp")
        self.chips = self.count // 2
        self.side = 1
        while 4 * self.side * self.side < self.chips:
            self.side *= 2
        self.device = lax.axis_index("dp")
        self.core = self.device % 2
        self.chip = self.device // 2

    def ring(self, array, by):
        step = 2 * self.side * self.side * by
        return lax.ppermute(
            array, "dp", [(i, (i + step) % self.count) for i in range(self.count)]
        )

    def chip_along(self, array, by):
        pairs = [(i, i + 2 * by) for i in range(self.count) if 0 <= i + 2 * by < self.count]
        return lax.ppermute(array, "dp", pairs)

    def last_core_along(self, array, by):
        pairs = [(i, i + 2 * by) for i in range(1, self.count, 2) if 0 <= i + 2 * by < self.count]
        return lax.ppermute(array, "dp", pairs)

    def pair(self, array):
        return lax.ppermute(array, "dp", [(i, i ^ 1) for i in range(self.count)])

    def plane(self, array, stage, amount):
        pairs = []
        for i in range(self.count):
            along_x = i % 2 != stage % 2
            pairs.append((i, i ^ (2 * amount * (1 if along_x else self.side))))
        return lax.ppermute(array, "dp", pairs)

    def by_core(self, mine, other, axis=0):
        return jnp.where(
            self.core == 0,
            jnp.concatenate([mine, other], axis=axis),
            jnp.concatenate([other, mine], axis=axis),
        )

    def places(self, chip, unit):
        side = self.side
        entry = jnp.arange(self.chips * unit, dtype=jnp.int32)
        inner, block = entry % unit, entry // unit
        along_z, first, second = block % 4, block // 4 % side, block // (4 * side)
        along_x = jnp.where(self.core == 0, second, first)
        along_y = jnp.where(self.core == 0, first, second)
        own_x, own_y, own_z = chip % side, chip // side % side, chip // (side * side)
        source = (
            ((own_z - along_z + 4) % 4) * side * side + (own_y ^ along_y) * side + (own_x ^ along_x)
        )
        return source * unit + inner

    def swapped(self, array):
        size = array.shape[1] // (self.side * self.side)
        starts = [
            (second * self.side + first) * size
            for first in range(self.side)
            for second in range(self.side)
        ]
        return jnp.concatenate([array[:, start : start + size] for start in starts], 1)

    def pair_in(self, array, count):
        return jnp.concatenate([self.pair(part) for part in jnp.split(array, count)])

    def scatter_z(self, blocks):
        return [blocks[0], blocks[1], self.ring(blocks[2], -1), self.ring(blocks[3], 1)]

    def scatter_z_last(self, terms):
        own, one, two, three = terms
        sent = (one.astype(full) + two.astype(full)).astype(one.dtype)
        return [own, three, self.ring(sent, -1)]

    def gather_plane(self, array, stage):
        return [array] + [self.plane(array, stage, m) for m in range(1, self.side)]

    def scatter_plane(self, parts, stage):
        return [self.plane(part, stage, m + 1) for m, part in enumerate(parts[1:])]


def place_kernel(core_ref, mine_ref, other_ref, out_ref):
    at_mine = pl.program_id(0) == core_ref[0]

    @pl.when(at_mine)
    def _():
        out_ref[...] = mine_ref[...]

    @pl.when(jnp.logical_not(at_mine))
    def _():
        out_ref[...] = other_ref[...]


def place(which, mine, other):
    rows, columns = mine.shape
    return call(
        place_kernel,
        "place",
        (2,),
        [whole_block(mine), whole_block(other)],
        [((2 * rows, columns), mine.dtype, mine.shape, lambda i, core: (i, 0))],
        0,
        8 * mine.size,
        scalars=(which,),
    )[0]


def fold_kernel(counts, core_ref, *refs):
    ins, (mine_ref, other_ref) = refs[:-2], refs[-2:]
    rows = mine_ref.shape[0]
    first = core_ref[0] == 0
    start, at = 0, 0
    for count in counts:
        terms = [ref[...].astype(full) for ref in ins[at : at + count]]
        total = sum(terms[1:], terms[0])
        here = slice(start, start + total.shape[1])
        mine_ref[:, here] = jnp.where(first, total[:rows], total[rows:])
        other_ref[:, here] = jnp.where(first, total[rows:], total[:rows])
        start += total.shape[1]
        at += count


def fold(which, *groups):
    rows = groups[0][0].shape[0] // 2
    columns = sum([group[0].shape[1] for group in groups])
    terms = [term for group in groups for term in group]
    fixed = lambda i, core: (0, 0)
    return call(
        functools.partial(fold_kernel, tuple([len(group) for group in groups])),
        "fold",
        (1,),
        [whole_block(term) for term in terms],
        [((rows, columns), full, (rows, columns), fixed)] * 2,
        0,
        20 * rows * columns,
        scalars=(which,),
    )


def join_kernel(ranges, core_ref, mine_ref, other_ref, *outs):
    def write(first, second):
        for out, spans in zip(outs, ranges):
            at = 0
            for ref in (first, second):
                for start, end in spans:
                    out[:, at : at + end - start] = ref[:, start:end]
                    at += end - start

    pl.when(core_ref[0] == 0)(lambda: write(mine_ref, other_ref))
    pl.when(core_ref[0] != 0)(lambda: write(other_ref, mine_ref))


def join(which, mine, other, *ranges):
    rows = mine.shape[0]
    widths = [2 * sum([end - start for start, end in spans]) for spans in ranges]
    fixed = lambda i, core: (0, 0)
    return call(
        functools.partial(join_kernel, ranges),
        "join",
        (1,),
        [whole_block(mine), whole_block(other)],
        [((rows, columns), mine.dtype, (rows, columns), fixed) for columns in widths],
        0,
        16 * mine.size,
        scalars=(which,),
    )


def cut_kernel(cuts, blocks, *refs):
    ins, outs = refs[:blocks], refs[blocks:]
    rows = ins[0].shape[0]
    for at, block in enumerate(ins):
        for out, start, end in zip(outs, cuts[:-1], cuts[1:]):
            out[at * rows : (at + 1) * rows, :] = block[:, start:end]


def stack_cut(blocks, cuts):
    rows, columns = blocks[0].shape
    cuts = (0,) + tuple(cuts) + (columns,)
    shapes = [
        (len(blocks) * rows, end - start) for start, end in zip(cuts[:-1], cuts[1:])
    ]
    return call(
        functools.partial(cut_kernel, cuts, len(blocks)),
        "stack_cut",
        (1,),
        [whole_block(block) for block in blocks],
        [(shape, low, shape, lambda i: (0, 0)) for shape in shapes],
        0,
        4 * len(blocks) * rows * columns,
    )


def score_bias(query_segments, key_segments, rows, halo):
    key_count, query_count = key_segments.shape[0], query_segments.shape[1]
    key_place = lax.broadcasted_iota(jnp.int32, (key_count, query_count), 0) - halo
    query_place = lax.broadcasted_iota(jnp.int32, (key_count, query_count), 1)
    seen = (key_segments == query_segments) & (key_place <= query_place)
    return jnp.where(seen, 0.0, -1e30).astype(full)


def parts_of(rows, halo):
    return (((0, halo), 2 * halo), ((halo, rows), halo + rows))


def reorder(refs, part, parts, unit):
    size = refs[0].shape[0] // parts
    return jnp.concatenate(
        [
            ref[row : row + unit, :]
            for row in range(part * size, (part + 1) * size, unit)
            for ref in refs
        ],
        axis=0,
    )


def write_parts(out_ref, parts, swap=False):
    side = parts.side
    for second in range(side):
        found = parts(second).astype(out_ref.dtype)
        width = found.shape[1]
        if not swap:
            out_ref[:, second * width : (second + 1) * width] = found
            continue
        size = width // side
        for first in range(side):
            start = (first * side + second) * size
            out_ref[:, start : start + size] = found[:, first * size : (first + 1) * size]


class Parts:
    def __init__(self, side, find):
        self.side = side
        self.find = find

    def __call__(self, part):
        return self.find(part)


def contract(value, refs, columns=slice(None)):
    size = refs[0].shape[0]
    total = None
    for at, ref in enumerate(refs):
        term = dot(value[:, at * size : (at + 1) * size], ref[:, columns])
        total = term if total is None else total + term
    return total


def turn(values, cosines, sines):
    return values * cosines + pltpu.roll(values, values.shape[1] // 2, 1) * sines


def row_rms(values):
    return lax.rsqrt(jnp.mean(values * values, axis=1, keepdims=True) + epsilon)


def call(
    kernel, name, grid, ins, outs, flops, bytes_accessed, scratch=(), transcendentals=0, scalars=(),
    least=0,
):
    size = sum([2 * math.prod(block) * array.dtype.itemsize for array, block, _ in ins])
    size += sum([2 * math.prod(block) * jnp.dtype(kind).itemsize for _, kind, block, _ in outs])
    size += sum([math.prod(part.shape) * jnp.dtype(part.dtype).itemsize for part in scratch])
    return pl.pallas_call(
        kernel,
        grid_spec=pltpu.PrefetchScalarGridSpec(
            num_scalar_prefetch=len(scalars),
            grid=grid,
            in_specs=[pl.BlockSpec(block, index) for _, block, index in ins],
            out_specs=[pl.BlockSpec(block, index) for _, _, block, index in outs],
            scratch_shapes=list(scratch),
        ),
        out_shape=[jax.ShapeDtypeStruct(shape, kind) for shape, kind, _, _ in outs],
        compiler_params=pltpu.CompilerParams(vmem_limit_bytes=max(size + (10 << 20), least)),
        cost_estimate=pl.CostEstimate(
            flops=flops, bytes_accessed=bytes_accessed, transcendentals=transcendentals
        ),
        name=name,
    )(*scalars, *[array for array, _, _ in ins])


def tile_of(columns):
    return next(tile for tile in (768, 512, 256, 128, columns) if columns % tile == 0)


def whole_block(array):
    return (array, array.shape, lambda *at: (0,) * array.ndim)


def project_kernel(q_cols, k_cols, x_ref, cos_ref, sin_ref, pick_ref, *refs):
    parts = refs[:-8]
    in_ref, q_ref, k_ref, v_ref, qp_ref, kp_ref, rows_ref, heads_ref = refs[-8:]
    head_size = heads_ref.shape[1]
    k_at = q_cols + 128
    step = pl.program_id(0)

    @pl.when(step == 0)
    def _():
        found = [ref[:, q_cols:k_at].astype(full).T[:8] for ref in parts]
        rows = jnp.concatenate(found, axis=1)
        rows_ref[...] = rows
        heads_ref[...] = dot(rows.astype(low), pick_ref[...])

    x = x_ref[...].astype(full)
    attn_in = (x * row_rms(x) * rows_ref[0:1, :]).astype(low)
    in_ref[...] = attn_in
    cosines, sines = cos_ref[...], sin_ref[...]

    def heads_of(projected, gain, proj_ref, out_ref, start):
        proj_ref[:, start : start + projected.shape[1]] = projected.astype(low)
        for column in range(0, projected.shape[1], head_size):
            head = projected[:, column : column + head_size]
            head = turn(head * row_rms(head) * gain, cosines, sines)
            out_ref[:, start + column : start + column + head_size] = head.astype(low)

    heads_of(contract(attn_in, parts, slice(k_at, k_at + k_cols)), heads_ref[3:4, :], kp_ref, k_ref, 0)
    v_ref[...] = contract(attn_in, parts, slice(k_at + k_cols, k_at + 2 * k_cols)).astype(low)

    @pl.when(step > 0)
    def _():
        for start in range(0, q_cols, 512):
            heads_of(
                contract(attn_in, parts, slice(start, start + 512)),
                heads_ref[2:3, :], qp_ref, q_ref, start,
            )


def project(ordered, cosines, sines, pick, parts, q_cols, k_cols, halo):
    row_count, width = ordered.shape
    own = row_count - halo
    head_size = cosines.shape[1]
    tile = lambda i: (i, 0)
    later = lambda i: (jnp.maximum(i - 1, 0), 0)
    fixed = lambda i: (0, 0)
    return call(
        functools.partial(project_kernel, q_cols, k_cols),
        "project",
        (row_count // halo,),
        [
            (ordered, (halo, width), tile),
            (cosines, (halo, head_size), tile),
            (sines, (halo, head_size), tile),
            whole_block(pick),
        ]
        + [whole_block(part) for part in parts],
        [
            ((row_count, width), low, (halo, width), tile),
            ((own, q_cols), low, (halo, q_cols), later),
            ((row_count, k_cols), low, (halo, k_cols), tile),
            ((row_count, k_cols), low, (halo, k_cols), tile),
            ((own, q_cols), low, (halo, q_cols), later),
            ((row_count, k_cols), low, (halo, k_cols), tile),
            ((8, width), full, (8, width), fixed),
            ((8, head_size), full, (8, head_size), fixed),
        ],
        2 * row_count * width * (q_cols + 2 * k_cols),
        20 << 20,
    )


def gate_kernel(side, xm_ref, xo_ref, *refs):
    first_refs, gate_refs, up_refs = refs[:side], refs[side : 2 * side], refs[2 * side : 3 * side]
    act_ref, to_gate_ref, to_up_ref = refs[3 * side :]
    half = xm_ref.shape[0]

    def write(gate_refs):
        for at, ref in enumerate((xm_ref, xo_ref)):
            rows = slice(at * half, (at + 1) * half)
            gate = contract(ref, gate_refs)
            up = contract(ref, up_refs)
            sigma = 1.0 / (1.0 + jnp.exp(-gate))
            silu = gate * sigma
            act_ref[rows, :] = (silu * up).astype(low)
            to_gate_ref[rows, :] = (up * sigma * (1.0 + gate * (1.0 - sigma))).astype(low)
            to_up_ref[rows, :] = silu.astype(low)

    pl.when(pl.program_id(0) == 0)(lambda: write(first_refs))
    pl.when(pl.program_id(0) == 1)(lambda: write(gate_refs))


def gate_forward(mine, other, mix, gate, up):
    half, width = mine.shape
    size, tile = gate[0].shape
    wide = lambda j: (0, j)
    fixed = lambda j: (0, 0)
    return call(
        functools.partial(gate_kernel, len(gate)),
        "gate_forward",
        (2,),
        [whole_block(mine), whole_block(other)]
        + [(part, (size, tile), fixed) for part in mix + gate]
        + [(part, (size, tile), wide) for part in up],
        [((2 * half, 2 * tile), low, (2 * half, tile), wide)] * 3,
        16 * half * width * tile,
        16 << 20,
        transcendentals=4 * half * tile,
    )


def act_back_kernel(unit, gb_ref, to_gate_ref, to_up_ref, *refs):
    down_refs, (gate_out, up_out) = refs[:4], refs[4:]
    act_grad = dot(gb_ref[...], reorder(down_refs, 0, 1, unit))
    gate_out[...] = (act_grad * to_gate_ref[...].astype(full)).astype(low)
    up_out[...] = (act_grad * to_up_ref[...].astype(full)).astype(low)


def act_backward(both, to_gate, to_up, down_parts, unit):
    rows, columns = to_gate.shape
    tile = min(tile_of(columns), 512)
    wide = lambda j: (0, j)
    return call(
        functools.partial(act_back_kernel, unit),
        "act_backward",
        (columns // tile,),
        [whole_block(both)]
        + [(factor, (rows, tile), wide) for factor in (to_gate, to_up)]
        + [(part, (part.shape[0], tile), wide) for part in down_parts],
        [((rows, columns), low, (rows, tile), wide)] * 2,
        2 * both.size * columns,
        16 << 20,
    )


def mlp_back_kernel(side, steps, gate_ref, up_ref, *refs):
    firsts, gates, ups = (refs[at * side : (at + 1) * side] for at in range(3))
    other_ref, mine_ref = refs[3 * side :]
    cut = gate_ref.shape[1] // 2
    found = Parts(
        side,
        lambda part: dot(gate_ref[:, :cut], firsts[part][...], 1, 1)
        + dot(gate_ref[:, cut:], gates[part][...], 1, 1)
        + dot(up_ref[...], ups[part][...], 1, 1),
    )
    pl.when(pl.program_id(0) < steps)(lambda: write_parts(other_ref, found, swap=True))
    pl.when(pl.program_id(0) >= steps)(lambda: write_parts(mine_ref, found))


def mlp_backward(gate_grad, up_grad, mix, gate, up, tile=256):
    rows, columns = gate_grad.shape[0] // 2, gate_grad.shape[1]
    size = gate[0].shape[0]
    width = len(gate) * size
    steps = rows // tile
    rows_of = lambda i: ((i + steps) % (2 * steps), 0)
    return call(
        functools.partial(mlp_back_kernel, len(gate), steps),
        "mlp_backward",
        (2 * steps,),
        [(grad, (tile, columns), rows_of) for grad in (gate_grad, up_grad)]
        + [(part, (size, columns // 2), lambda i: (0, 0)) for part in mix]
        + [whole_block(part) for part in gate + up],
        [
            ((rows, width), full, (tile, width), lambda i: (jnp.minimum(i, steps - 1), 0)),
            ((rows, width), full, (tile, width), lambda i: (jnp.maximum(i - steps, 0), 0)),
        ],
        1,
        1,
    )


def down_kernel(side, unit, steps, act_ref, *refs):
    down_refs, (other_ref, mine_ref) = refs[:4], refs[4:]
    parts = Parts(
        side, lambda part: dot(act_ref[...], reorder(down_refs, part, side, unit), 1, 1)
    )
    pl.when(pl.program_id(0) < steps)(lambda: write_parts(other_ref, parts, swap=True))
    pl.when(pl.program_id(0) >= steps)(lambda: write_parts(mine_ref, parts))


def down_forward(activated, down_parts, side, unit, tile=256):
    rows, columns = activated.shape[0] // 2, activated.shape[1]
    width = 4 * down_parts[0].shape[0]
    steps = rows // tile
    return call(
        functools.partial(down_kernel, side, unit, steps),
        "down_forward",
        (2 * steps,),
        [(activated, (tile, columns), lambda i: ((i + steps) % (2 * steps), 0))]
        + [whole_block(part) for part in down_parts],
        [
            ((rows, width), full, (tile, width), lambda i: (jnp.minimum(i, steps - 1), 0)),
            ((rows, width), full, (tile, width), lambda i: (jnp.maximum(i - steps, 0), 0)),
        ],
        1,
        1,
    )


def back_kernel(side, q_cols, steps, core_ref, q_ref, k_ref, v_ref, halo_ref, *refs):
    parts, (other_ref, mine_ref) = refs[:side], refs[side:]
    step = pl.program_id(0)
    k_cols = k_ref.shape[1]
    k_at = q_cols + 128
    v_at = k_at + k_cols
    half = jnp.where(step < steps, 1 - core_ref[0], core_ref[0])
    last = (half == 1) & (step % steps == steps - 1)
    later = jnp.where(last, halo_ref[...].astype(full), 0.0)
    keys = (k_ref[...].astype(full) + later[:, :k_cols]).astype(low)
    values = (v_ref[...].astype(full) + later[:, k_cols:]).astype(low)

    def terms(part):
        return (
            dot(q_ref[...], parts[part][:, :q_cols], 1, 1)
            + dot(keys, parts[part][:, k_at:v_at], 1, 1)
            + dot(values, parts[part][:, v_at : v_at + k_cols], 1, 1)
        )

    pl.when(step < steps)(lambda: write_parts(other_ref, Parts(side, terms), swap=True))
    pl.when(step >= steps)(lambda: write_parts(mine_ref, Parts(side, terms)))


def input_backward(which, query_low, key_low, value_low, later, parts):
    own, q_cols = query_low.shape
    k_cols = key_low.shape[1]
    tile = later.shape[0]
    halo_steps = (key_low.shape[0] - own) // tile
    steps = own // 2 // tile
    width = len(parts) * parts[0].shape[0]

    def own_rows(i, core):
        half = jnp.where(i < steps, 1 - core[0], core[0])
        return half * steps + i % steps

    return call(
        functools.partial(back_kernel, len(parts), q_cols, steps),
        "input_backward",
        (2 * steps,),
        [(query_low, (tile, q_cols), lambda i, core: (own_rows(i, core), 0))]
        + [
            (part, (tile, k_cols), lambda i, core: (halo_steps + own_rows(i, core), 0))
            for part in (key_low, value_low)
        ]
        + [whole_block(part) for part in [later] + parts],
        [
            ((own // 2, width), full, (tile, width), lambda i, core: (jnp.minimum(i, steps - 1), 0)),
            ((own // 2, width), full, (tile, width), lambda i, core: (jnp.maximum(i - steps, 0), 0)),
        ],
        1,
        1,
        scalars=(which,),
    )


def finish_kernel(core_ref, mine_ref, sent_ref, x_ref, hidden_ref, gain_ref, out_ref, sum_ref):
    grad = mine_ref[...] + sent_ref[...]
    x = x_ref[...].astype(full)
    scales = row_rms(x)
    normed = x * scales

    @pl.when(pl.program_id(0) == 0)
    def _():
        sum_ref[...] = jnp.zeros_like(sum_ref)

    sum_ref[0:1, :] += jnp.sum(grad * normed, axis=0, keepdims=True)
    back = grad * gain_ref[0:1, :]
    mean = jnp.mean(back * normed, axis=1, keepdims=True)
    out_ref[...] = (hidden_ref[...] + scales * (back - normed * mean)).astype(low)


def finish_tokens(which, mine, sent, inputs, hidden_grad, gains, tile=128):
    rows, width = mine.shape
    rows_of = lambda i, core: (i, 0)
    fixed = lambda i, core: (0, 0)
    before = (inputs.shape[0] - 2 * rows) // tile
    later = lambda i, core: (before + core[0] * (rows // tile) + i, 0)
    block = (tile, width)
    return call(
        finish_kernel,
        "finish_tokens",
        (rows // tile,),
        [(mine, block, rows_of), (sent, block, rows_of), (inputs, block, later)]
        + [(hidden_grad, block, rows_of), whole_block(gains)],
        [((rows, width), low, block, rows_of), ((8, width), full, (8, width), fixed)],
        1,
        1,
        scalars=(which,),
    )


def sums_kernel(side, groups, segments, *refs):
    outs, turned = refs[-1 - side * groups : -1], refs[-1]
    right_refs = refs[-1 - side * groups - len(segments) : -1 - side * groups]
    left_refs = refs[: -1 - side * groups - len(segments)]
    step = pl.program_id(0)
    size = turned.shape[0] // side

    @pl.when(step == 0)
    def _():
        start = 0
        for ref in left_refs:
            turned[:, start : start + ref.shape[0]] = ref[...].T
            start += ref.shape[0]

    for ref, (first, steps, row, group) in zip(right_refs, segments):

        @pl.when((step >= first) & (step < first + steps))
        def _(ref=ref, row=row, group=group):
            for part, out in enumerate(outs[group * side : (group + 1) * side]):
                out[...] = dot(turned[part * size : (part + 1) * size, row:], ref[...]).astype(low)


def token_sums(side, lefts, *groups):
    width = lefts[0].shape[1]
    tokens = sum([left.shape[0] for left in lefts])
    tile = min([tile_of(array.shape[1]) for group in groups for array, _ in group])
    segments, step, ins, outs = [], 0, [], []

    def clip(first, steps):
        return lambda j: (0, jnp.clip(j - first, 0, steps - 1))

    for at, group in enumerate(groups):
        begin = step
        for array, row in group:
            steps = array.shape[1] // tile
            segments.append((step, steps, row, at))
            ins.append((array, (array.shape[0], tile), clip(step, steps)))
            step += steps
        block = (width // side, tile)
        shape = (width // side, (step - begin) * tile)
        outs += [(shape, low, block, clip(begin, step - begin))] * side
    found = call(
        functools.partial(sums_kernel, side, len(groups), tuple(segments)),
        "token_sums",
        (step,),
        [whole_block(left) for left in lefts] + ins,
        outs,
        1,
        1,
        scratch=[pltpu.VMEM((width, tokens), low)],
    )
    return [list(found[at * side : (at + 1) * side]) for at in range(len(groups))]


def mix_kernel(side, steps, core_ref, att_left, att_right, *refs):
    weights, (other_ref, mine_ref) = refs[:side], refs[side:]
    cut = att_left.shape[1]
    start = weights[0].shape[1] - 2 * cut
    parts = Parts(
        side,
        lambda part: dot(att_left[...], weights[part][:, start : start + cut], 1, 1)
        + dot(att_right[...], weights[part][:, start + cut :], 1, 1),
    )
    pl.when(pl.program_id(0) < steps)(lambda: write_parts(other_ref, parts, swap=True))
    pl.when(pl.program_id(0) >= steps)(lambda: write_parts(mine_ref, parts))


def mix_forward(which, att_left, att_right, weights, tile=256):
    rows, columns = att_left.shape[0] // 2, att_left.shape[1]
    width = len(weights) * weights[0].shape[0]
    steps = rows // tile

    def rows_of(i, core):
        half = jnp.where(i < steps, 1 - core[0], core[0])
        return (half * steps + i % steps, 0)

    return call(
        functools.partial(mix_kernel, len(weights), steps),
        "mix_forward",
        (2 * steps,),
        [(part, (tile, columns), rows_of) for part in (att_left, att_right)]
        + [whole_block(part) for part in weights],
        [
            ((rows, width), full, (tile, width), lambda i, core: (jnp.minimum(i, steps - 1), 0)),
            ((rows, width), full, (tile, width), lambda i, core: (jnp.maximum(i - steps, 0), 0)),
        ],
        1,
        1,
        scalars=(which,),
    )


def mix_back_kernel(branch_ref, *refs):
    weights, out_ref = refs[:-1], refs[-1]
    start = weights[0].shape[1] - out_ref.shape[1]
    out_ref[...] = contract(branch_ref, weights, slice(start, None)).astype(low)


def mix_backward(branch, weights, columns, tile=256):
    rows, width = branch.shape
    rows_of = lambda i: (i, 0)
    return call(
        mix_back_kernel,
        "mix_backward",
        (rows // tile,),
        [(branch, (tile, width), rows_of)] + [whole_block(part) for part in weights],
        [((rows, columns), low, (tile, columns), rows_of)],
        1,
        1,
    )[0]


def forward_kernel(scale, rows, halo, q_ref, k_ref, v_ref, qs_ref, ks_ref, out_ref, bias_ref):
    block = pl.program_id(1)
    start = pl.multiple_of(block * rows, rows)
    window = halo + rows
    head_size = k_ref.shape[1]

    @pl.when(pl.program_id(0) == 0)
    def _():
        bias_ref[block] = score_bias(
            qs_ref[...], ks_ref[pl.ds(start, window), :], rows, halo
        )

    for (low_row, high_row), key_count in parts_of(rows, halo):
        keys = k_ref[pl.ds(start, key_count), :]
        values = v_ref[pl.ds(start, key_count), :]
        bias = bias_ref[block, :key_count, low_row:high_row]
        for group in range(q_ref.shape[1] // head_size):
            lanes = slice(group * head_size, (group + 1) * head_size)
            query = q_ref[low_row:high_row, lanes]
            scores = dot(keys, query, 1, 1) * scale + bias
            weights = jnp.exp2(scores)
            total = jnp.sum(weights, axis=0, keepdims=True)
            probs = (weights * (1.0 / total)).astype(low)
            mixed = dot(values, probs, 0, 0)
            out_ref[low_row:high_row, lanes] = mixed.T.astype(low)


def head_back(gradient, projected, gain, cosines, sines):
    scales = row_rms(projected)
    normed = projected * scales
    back = turn(gradient, cosines, -sines)
    gain_grad = jnp.sum(back * normed, axis=0, keepdims=True)
    back = back * gain
    mean = jnp.mean(back * normed, axis=1, keepdims=True)
    return scales * (back - normed * mean), gain_grad


def backward_kernel(
    scale, rows, halo, *refs
):
    q_ref, k_ref, v_ref, g_ref, qp_ref, kp_ref, cos_ref, sin_ref, heads_ref, qs_ref, ks_ref = refs[
        :11
    ]
    dq_ref, dk_ref, dv_ref, gains_ref, bias_ref, key_ref, value_ref = refs[11:]
    head = pl.program_id(0)
    block = pl.program_id(1)
    start = pl.multiple_of(block * rows, rows)
    window = halo + rows
    head_size = k_ref.shape[1]
    factor = head_size ** (-0.5)

    @pl.when(head == 0)
    def _():
        bias_ref[block] = score_bias(
            qs_ref[...], ks_ref[pl.ds(start, window), :], rows, halo
        )

    @pl.when((head == 0) & (block == 0))
    def _():
        gains_ref[...] = jnp.zeros_like(gains_ref)

    @pl.when(block == 0)
    def _():
        key_ref[...] = jnp.zeros_like(key_ref)
        value_ref[...] = jnp.zeros_like(value_ref)

    for (low_row, high_row), key_count in parts_of(rows, halo):
        keys = k_ref[pl.ds(start, key_count), :]
        values = v_ref[pl.ds(start, key_count), :]
        bias = bias_ref[block, :key_count, low_row:high_row]
        here = pl.ds(start + (halo + low_row), high_row - low_row)
        cosines, sines = cos_ref[here, :], sin_ref[here, :]
        key_sum = None
        value_sum = None
        for group in range(q_ref.shape[1] // head_size):
            lanes = slice(group * head_size, (group + 1) * head_size)
            query = q_ref[low_row:high_row, lanes]
            grad = g_ref[low_row:high_row, lanes]
            weights = jnp.exp2(dot(keys, query, 1, 1) * scale + bias)
            total = jnp.sum(weights, axis=0, keepdims=True)
            softmax = weights * (1.0 / total)
            prob_grad = dot(values, grad, 1, 1)
            product = softmax * prob_grad
            mean = jnp.sum(product, axis=0, keepdims=True)
            score_grad = (product - softmax * mean).astype(low)
            value_term = dot(softmax.astype(low), grad)
            key_term = dot(score_grad, query)
            value_sum = value_term if value_sum is None else value_sum + value_term
            key_sum = key_term if key_sum is None else key_sum + key_term
            query_grad = dot(keys, score_grad, 0, 0).T * factor
            query_grad, gain_grad = head_back(
                query_grad,
                qp_ref[low_row:high_row, lanes].astype(full),
                heads_ref[2:3, :],
                cosines,
                sines,
            )
            dq_ref[low_row:high_row, lanes] = query_grad.astype(low)
            gains_ref[0:1, :] += gain_grad
        key_ref[pl.ds(start, key_count), :] += key_sum * factor
        value_ref[pl.ds(start, key_count), :] += value_sum

    @pl.when(block == pl.num_programs(1) - 1)
    def _():
        dv_ref[...] = value_ref[...].astype(low)
        for row in range(0, k_ref.shape[0], halo):
            here = slice(row, row + halo)
            key_grad, gain_grad = head_back(
                key_ref[here, :],
                kp_ref[here, :].astype(full),
                heads_ref[3:4, :],
                cos_ref[here, :],
                sin_ref[here, :],
            )
            dk_ref[here, :] = key_grad.astype(low)
            gains_ref[1:2, :] += gain_grad


def attention_forward(
    queries, keys, values, query_segments, key_segments, rows, halo, head_size, first, heads
):
    token_count = queries.shape[0]
    lanes = queries.shape[1] // (keys.shape[1] // head_size)
    window = halo + token_count
    scale = head_size ** (-0.5) / math.log(2.0)
    q_at, k_at = lambda h, b: (b, first + h), lambda h, b: (0, first + h)
    shape = (token_count, heads * lanes)
    return call(
        functools.partial(forward_kernel, scale, rows, halo),
        "attention_forward",
        (heads, token_count // rows),
        [
            (queries, (rows, lanes), q_at),
            (keys, (window, head_size), k_at),
            (values, (window, head_size), k_at),
            (query_segments, (1, rows), lambda h, b: (0, b)),
            whole_block(key_segments),
        ],
        [(shape, low, (rows, lanes), lambda h, b: (b, h))],
        4 * token_count * heads * lanes * (halo + rows),
        4 << 20,
        scratch=[pltpu.VMEM((token_count // rows, halo + rows, rows), full)],
        transcendentals=token_count * heads * lanes // head_size * (halo + rows),
    )[0]


def attention_backward(
    queries, keys, values, grads, query_proj, key_proj, cosines, sines, heads_gain,
    query_segments, key_segments, rows, halo, head_size,
):
    token_count = queries.shape[0]
    heads = keys.shape[1] // head_size
    lanes = queries.shape[1] // heads
    window = halo + token_count
    scale = head_size ** (-0.5) / math.log(2.0)
    q_at, k_at, fixed = lambda h, b: (b, h), lambda h, b: (0, h), lambda h, b: (0, 0)
    return call(
        functools.partial(backward_kernel, scale, rows, halo),
        "attention_backward",
        (heads, token_count // rows),
        [
            (queries, (rows, lanes), q_at),
            (keys, (window, head_size), k_at),
            (values, (window, head_size), k_at),
            (grads, (rows, lanes), q_at),
            (query_proj, (rows, lanes), q_at),
            (key_proj, (window, head_size), k_at),
            whole_block(cosines),
            whole_block(sines),
            whole_block(heads_gain),
            (query_segments, (1, rows), lambda h, b: (0, b)),
            whole_block(key_segments),
        ],
        [
            (queries.shape, low, (rows, lanes), q_at),
            (keys.shape, low, (window, head_size), k_at),
            (keys.shape, low, (window, head_size), k_at),
            ((8, head_size), full, (8, head_size), fixed),
        ],
        10 * queries.size * (halo + rows),
        24 << 20,
        scratch=[
            pltpu.VMEM((token_count // rows, halo + rows, rows), full),
            pltpu.VMEM((window, head_size), full),
            pltpu.VMEM((window, head_size), full),
        ],
        least=48 << 20,
        transcendentals=queries.size // head_size * (halo + rows),
    )


def per_device(
    tokens,
    segments,
    norm_gain,
    q_weight,
    k_weight,
    v_weight,
    o_weight,
    q_gain,
    k_gain,
    mlp_gain,
    gate_weight,
    up_weight,
    down_weight,
    cotangent,
):
    net = Slice()
    row_count, width = tokens.shape
    halo = row_count // 2
    chip_rows = 2 * row_count
    weight_rows = q_weight.shape[0]
    head_size = q_gain.shape[0] * net.count
    gain_rows = q_gain.shape[0]

    q_cols, k_cols, o_cols, ff_cols = (
        weight.shape[1] // 2 for weight in (q_weight, k_weight, o_weight, gate_weight)
    )
    ff_cut = ff_cols // 2
    unit = 2 * weight_rows
    side = net.side
    which = net.core.astype(jnp.int32).reshape(1)

    column = lax.broadcasted_iota(jnp.int32, (weight_rows, 128), 1)
    extras = jnp.zeros((weight_rows, 128), low)
    for at, gain in enumerate((norm_gain, mlp_gain, q_gain, k_gain)):
        gain = jnp.pad(gain, (0, weight_rows - gain.shape[0]))
        extras = jnp.where(column == at, gain[:, None], extras)

    def chip_block(*parts):
        mine, other = [], []
        for weight, start, end in parts:
            half = weight.shape[1] // 2 if end is not None else 0
            for to, core in ((mine, net.core), (other, 1 - net.core)):
                if end is None:
                    to.append(weight)
                else:
                    to.append(
                        lax.dynamic_slice_in_dim(weight, core * half + start, end - start, 1)
                    )
        return net.by_core(jnp.concatenate(mine, 1), net.pair(jnp.concatenate(other, 1)))

    block_qkv = chip_block(
        (q_weight, 0, q_cols), (extras, 0, None), (k_weight, 0, k_cols), (v_weight, 0, k_cols)
    )
    z_qkv = [block_qkv] + [net.ring(block_qkv, m) for m in range(1, 4)]
    numbers = jnp.broadcast_to(segments.astype(low)[:, None], (row_count, 128))
    own_tokens = jnp.concatenate([tokens, numbers], 1)
    before = net.last_core_along(own_tokens[row_count - halo :], 1)
    z_qkv, own_tokens, before, o_weight, gate_weight, up_weight, down_weight = barrier(
        (z_qkv, own_tokens, before, o_weight, gate_weight, up_weight, down_weight)
    )

    (qkv,) = stack_cut(z_qkv, ())
    qkv = net.gather_plane(qkv, 0)
    block_rest = chip_block(
        (down_weight, 0, ff_cols), (gate_weight, 0, ff_cut), (o_weight, 0, o_cols),
        (gate_weight, ff_cut, ff_cols), (up_weight, 0, ff_cols),
    )
    mix_end = ff_cols + ff_cut + o_cols
    block_down, block_mix, block_mlp = (
        block_rest[:, :ff_cols], block_rest[:, ff_cols:mix_end], block_rest[:, mix_end:]
    )
    z_mix = [block_mix, net.ring(block_mix, 1)]
    places = net.places(net.chip, unit)
    order = (jnp.arange(width, dtype=jnp.int32)[:, None] == places[None, :]).astype(low)
    head_places = net.places(net.chip, 2 * gain_rows)
    head_order = (
        jnp.arange(head_size, dtype=jnp.int32)[:, None] == head_places[None, :]
    ).astype(full)
    entry = jnp.arange(width, dtype=jnp.int32)
    gain_place = places // weight_rows * gain_rows + entry % weight_rows
    pick = (
        (entry % weight_rows < gain_rows)[:, None]
        & (gain_place[:, None] == jnp.arange(head_size, dtype=jnp.int32)[None, :])
    ).astype(low)
    plane_down = jnp.stack(net.gather_plane(block_down, 0))
    qkv, plane_down, own_tokens, before, order, pick, z_mix, block_mlp, cotangent = barrier(
        (qkv, plane_down, own_tokens, before, order, pick, z_mix, block_mlp, cotangent)
    )

    (qkv,) = stack_cut(qkv, ())
    qkv = net.gather_plane(qkv, 1)
    z_mix.append(net.ring(z_mix[-1], 1))
    z_mix.append(net.ring(z_mix[-1], 1))
    z_mlp = [block_mlp]
    for _ in range(3):
        z_mlp.append(net.ring(z_mlp[-1], 1))
    plane_down = jnp.stack(net.gather_plane(plane_down, 1))
    plane_down = plane_down.reshape(side * side * unit, ff_cols)
    both = place(which, own_tokens, net.pair(own_tokens))
    before = jnp.where(net.core == 0, net.pair(before), before)
    chip_tokens, before_tokens = both[:, :width], before[:, :width]
    chip_segments = both[:, width].astype(jnp.int32)
    before_segments = jnp.where(net.chip > 0, before[:, width].astype(jnp.int32), -1)
    window_tokens = jnp.concatenate([before_tokens, chip_tokens])
    window_segments = jnp.concatenate([before_segments, chip_segments])
    counter = jnp.arange(halo + chip_rows, dtype=jnp.int32)
    changes = jnp.concatenate([jnp.ones((1,), bool), window_segments[1:] != window_segments[:-1]])
    starts = lax.cummax(jnp.where(changes, counter, 0), axis=0)
    offsets = (counter - starts).astype(full)
    frequency = jnp.exp(
        (jnp.arange(head_size, dtype=jnp.int32) % (head_size // 2)).astype(full)
        * (-2.0 * math.log(rope_base) / head_size)
    )
    angles = offsets[:, None] * frequency[None, :]
    cosines = jnp.cos(angles)
    sines = jnp.sin(angles) * jnp.where(jnp.arange(head_size) < head_size // 2, -1.0, 1.0)
    query_segments = chip_segments[None, :]
    key_segments = window_segments[:, None]
    ordered = dot(window_tokens, order, kind=low)
    qkv, z_mix, z_mlp, plane_down, ordered, cosines, sines = barrier(
        (qkv, z_mix, z_mlp, plane_down, ordered, cosines, sines)
    )

    own_cotangent = dot(cotangent, order, kind=low)
    (mix,) = stack_cut(z_mix, ())
    mix = net.gather_plane(mix, 0)
    (mlp,) = stack_cut(z_mlp, ())
    mlp = net.gather_plane(mlp, 0)
    z_down = [plane_down, net.ring(plane_down, 1)]
    attn_in, queries, keys, values, query_proj, key_proj, gain_rows_full, heads_gain = project(
        ordered, cosines, sines, pick, qkv, q_cols, k_cols, halo
    )
    gain_one, gain_two = gain_rows_full[0], gain_rows_full[1]
    kv_heads = k_cols // head_size

    def attend(first):
        return attention_forward(
            queries, keys, values, query_segments, key_segments, row_count, halo, head_size,
            first, kv_heads // 2,
        )

    att_left = attend(0)
    att_left, mix, mlp, z_down, queries, keys, values, own_cotangent = barrier(
        (att_left, mix, mlp, z_down, queries, keys, values, own_cotangent)
    )

    other_cotangent = net.pair(net.swapped(own_cotangent))
    cotangents = jnp.concatenate([own_cotangent, other_cotangent])
    (mix,) = stack_cut(mix, ())
    mix = net.gather_plane(mix, 1)
    gate, up = stack_cut(mlp, (ff_cut,))
    att_right = attend(kv_heads // 2)
    z_down.append(net.ring(z_down[-1], 1))
    att_left, att_right, mix, gate, up, cotangents, z_down = barrier(
        (att_left, att_right, mix, gate, up, cotangents, z_down)
    )

    gate = net.gather_plane(gate, 1)
    branch_other, branch_mine = mix_forward(which, att_left, att_right, mix)
    branch_sent = net.pair_in(branch_other, 4)
    branch_mine, branch_sent, gate, up = barrier((branch_mine, branch_sent, gate, up))

    up = net.gather_plane(up, 1)
    z_down.append(net.ring(z_down[-1], 1))
    own_inputs = lax.dynamic_slice_in_dim(ordered, halo + net.core * row_count, row_count)
    hidden_state = own_inputs.astype(full) + (branch_mine + branch_sent)
    scale_two = inverse_rms(hidden_state)
    normed_two = hidden_state * scale_two
    mlp_own = (normed_two * gain_two).astype(low)
    mlp_other = net.pair_in(net.swapped(mlp_own), 2)
    mlp_own, mlp_other, up, z_down = barrier((mlp_own, mlp_other, up, z_down))

    activated, to_gate, to_up = gate_forward(mlp_own, mlp_other, mix, gate, up)
    (down_sums,) = token_sums(side, [cotangents], [(activated, 0)])
    activated, to_gate, to_up, down_sums, z_down = barrier(
        (activated, to_gate, to_up, down_sums, z_down)
    )

    def plus(array, *terms):
        return sum([term.astype(full) for term in terms], array.astype(full)).astype(array.dtype)

    def inner(terms):
        size = terms[0].shape[0] // side
        sent = [
            plus(*[term[at * size : (at + 1) * size] for term in terms]) for at in range(1, side)
        ]
        return terms, [None] + sent

    def kept(terms, received):
        size = received[0].shape[0]
        return plus(*[term[:size] for term in terms], *received)

    down_in = net.scatter_plane(down_sums, 1)
    gate_grad, up_grad = act_backward(cotangents, to_gate, to_up, z_down, unit)
    gate_sums, up_sums = token_sums(
        side, [mlp_own, mlp_other], [(gate_grad, 0)], [(up_grad, 0)]
    )
    gate_grad, up_grad, gate_sums, up_sums, down_sum, activated = barrier(
        (gate_grad, up_grad, gate_sums, up_sums, down_sums[:1] + down_in, activated)
    )

    gate_in = net.scatter_plane(gate_sums, 1)
    z_down_sum = plus(*down_sum).reshape(side, 4, unit, ff_cols)
    z_down_sum = [z_down_sum[:, m] for m in range(4)]
    mlp_grad_other, mlp_grad_mine = mlp_backward(gate_grad, up_grad, mix, gate, up)
    mlp_grad_sent = net.pair_in(mlp_grad_other, 4)
    out_other, out_mine = down_forward(activated, z_down, side, unit)
    mlp_grad_mine, mlp_grad_sent, gate_sum, up_sums, out_other, out_mine = barrier(
        (mlp_grad_mine, mlp_grad_sent, gate_sums[:1] + gate_in, up_sums, out_other, out_mine)
    )

    up_in = net.scatter_plane(up_sums, 1)
    out_sent = net.pair_in(out_other, 4)
    mixed_out = (hidden_state + (out_mine + out_sent)).astype(low)
    mixed_out = dot(mixed_out, order, 1, 1, low)
    gate_sum, gate_sent = inner(gate_sum)
    mlp_in_grad = mlp_grad_mine + mlp_grad_sent
    hidden_grad = own_cotangent.astype(full) + norm_back(
        mlp_in_grad * gain_two, normed_two, scale_two
    )
    branch_own = hidden_grad.astype(low)
    branch_low = place(which, branch_own, net.pair_in(net.swapped(branch_own), 2))
    attended_grad = mix_backward(branch_low, mix, o_cols)
    (mix_sums,) = token_sums(side, [branch_low], [(att_left, 0), (att_right, 0)])
    (
        attended_grad, mix_sums, mlp_in_grad, gate_sum, gate_sent, up_sum, z_down_sum, mixed_out
    ) = barrier(
        (
            attended_grad, mix_sums, mlp_in_grad, gate_sum, gate_sent, up_sums[:1] + up_in,
            z_down_sum, mixed_out,
        )
    )
    z_down_sum = net.scatter_z(z_down_sum)

    up_sum, up_sent = inner(up_sum)
    mlp_sent = [None] + [
        jnp.concatenate(both, 1) for both in zip(gate_sent[1:], up_sent[1:])
    ]
    mlp_in = net.scatter_plane(mlp_sent, 0)
    mix_in = net.scatter_plane(mix_sums, 1)
    query_low, key_low, value_low, gain_grads = attention_backward(
        queries, keys, values, attended_grad, query_proj, key_proj, cosines, sines, heads_gain,
        query_segments, key_segments, row_count, halo, head_size,
    )
    query_low, key_low, value_low, mlp_sum, mix_sum, z_down_sum = barrier(
        (
            query_low, key_low, value_low, (gate_sum, up_sum, mlp_in), mix_sums[:1] + mix_in,
            z_down_sum,
        )
    )

    mix_sum, mix_sent = inner(mix_sum)
    mix_in = net.scatter_plane(mix_sent, 0)
    z_down_sum = net.scatter_z_last(z_down_sum)
    later = net.chip_along(jnp.concatenate([key_low[:halo], value_low[:halo]], 1), -1)
    (qkv_sums,) = token_sums(
        side, [attn_in], [(query_low, halo), (key_low, 0), (value_low, 0)]
    )
    qkv_sums, query_low, mlp_in_grad, mix_sum, mlp_sum, z_down_sum, later = barrier(
        (qkv_sums, query_low, mlp_in_grad, (mix_sum, mix_in), mlp_sum, z_down_sum, later)
    )

    qkv_in = net.scatter_plane(qkv_sums, 1)
    gate_sum, up_sum, mlp_in = mlp_sum
    mlp_sum = jnp.concatenate(
        [
            kept(gate_sum, [part[:, :ff_cols] for part in mlp_in]),
            kept(up_sum, [part[:, ff_cols:] for part in mlp_in]),
        ],
        1,
    )
    z_mlp = net.scatter_z(jnp.split(mlp_sum, 4))
    gain_two_grad = jnp.sum(mlp_in_grad * normed_two, axis=0, keepdims=True)
    head_gains = dot(gain_grads[:2], head_order)
    z_mix = net.scatter_z(jnp.split(kept(*mix_sum), 4))
    z_mlp, z_mix, query_low, later = barrier((z_mlp, z_mix, query_low, later))
    grad_other, grad_mine = input_backward(which, query_low, key_low, value_low, later, qkv)
    qkv_sum, z_mlp, z_mix, gain_two_grad, head_gains, grad_other, grad_mine = barrier(
        (
            qkv_sums[:1] + qkv_in, z_mlp, z_mix, gain_two_grad, head_gains, grad_other, grad_mine,
        )
    )

    qkv_sum, qkv_sent = inner(qkv_sum)
    qkv_in = net.scatter_plane(qkv_sent, 0)
    z_mlp = net.scatter_z_last(z_mlp)
    z_mix = net.scatter_z_last(z_mix)
    down_sum = plus(*z_down_sum)
    down_in = net.scatter_plane([down_sum[m] for m in range(side)], 0)
    grad_sent = net.pair_in(grad_other, 4)
    input_grad, gain_one_grad = finish_tokens(
        which, grad_mine, grad_sent, ordered, hidden_grad, gain_rows_full
    )
    qkv_sum, z_mlp, z_mix, input_grad, gain_one_grad, down_sum = barrier(
        (
            (qkv_sum, qkv_in), z_mlp, z_mix, input_grad, gain_one_grad, [down_sum[0]] + down_in,
        )
    )

    z_qkv = net.scatter_z(jnp.split(kept(*qkv_sum), 4))
    input_grad = dot(input_grad, order, 1, 1, low)

    def blocks_of(count):
        return [
            jnp.concatenate(both, 1)
            for both in zip(jnp.split(gains, count, 1), jnp.split(heads, count, 1))
        ]

    def cut_gains(array):
        at = array.shape[1] * width // (width + head_size)
        return array[:, :at], array[:, at:]

    gains, heads = jnp.concatenate([gain_one_grad[:1], gain_two_grad]), head_gains
    gain_blocks = blocks_of(side)
    gain_blocks = [gain_blocks[0]] + net.scatter_plane(gain_blocks, 1)
    gains, heads = cut_gains(plus(*gain_blocks))
    gain_blocks = blocks_of(side)
    gain_blocks = [gain_blocks[0]] + net.scatter_plane(gain_blocks, 0)
    rest_mine, rest_other = fold(which, z_mlp, z_mix, down_sum)
    rest_other = net.pair(rest_other)
    z_qkv, gain_blocks, input_grad, rest_mine, rest_other = barrier(
        (z_qkv, gain_blocks, input_grad, rest_mine, rest_other)
    )

    z_qkv = net.scatter_z_last(z_qkv)
    gains, heads = cut_gains(plus(*gain_blocks))
    gain_blocks = blocks_of(4)
    gain_blocks = [gain_blocks[0]] + [net.ring(gain_blocks[m], -m) for m in range(1, 4)]
    z_qkv, gain_blocks = barrier((z_qkv, gain_blocks))

    z_mine, z_other = fold(which, z_qkv)
    z_other = net.pair(z_other)
    gains, heads = cut_gains(plus(*gain_blocks))
    gains = jnp.concatenate(
        [gains[:1, :weight_rows], gains[1:, :weight_rows], heads[:1, :gain_rows],
         heads[1:, :gain_rows], gains[:1, weight_rows:], gains[1:, weight_rows:],
         heads[:1, gain_rows:], heads[1:, gain_rows:]], 1,
    ).reshape(2, -1)
    gain_mine = jnp.where(net.core == 0, gains[0], gains[1])
    gain_other = jnp.where(net.core == 0, gains[1], gains[0])
    gain_sum = gain_mine + net.pair(gain_other)
    ends = [0]
    for size in (ff_cols, ff_cols, o_cols, ff_cols):
        ends.append(ends[-1] + size)
    gate_out, up_out, o_out, down_out = join(
        which, rest_mine, rest_other, *[((start, end),) for start, end in zip(ends[:-1], ends[1:])]
    )
    v_at = q_cols + k_cols
    q_out, k_out, v_out = join(
        which, z_mine, z_other, ((0, q_cols),), ((q_cols, v_at),), ((v_at, v_at + k_cols),)
    )
    return (
        mixed_out,
        input_grad,
        gain_sum[:weight_rows],
        q_out,
        k_out,
        v_out,
        o_out,
        gain_sum[2 * weight_rows : 2 * weight_rows + gain_rows],
        gain_sum[2 * weight_rows + gain_rows :],
        gain_sum[weight_rows : 2 * weight_rows],
        gate_out,
        up_out,
        down_out,
    )


def solution(mesh):
    rows = P("dp", None)
    line = P("dp")
    return jax.shard_map(
        per_device,
        mesh=mesh,
        in_specs=(
            rows, line, line, rows, rows, rows, rows, line, line, line, rows, rows, rows, rows,
        ),
        out_specs=(
            rows, rows, line, rows, rows, rows, rows, line, line, line, rows, rows, rows,
        ),
        check_vma=False,
    )
```
